128 devices in a mesh: adapter: 16 (over y, z), tensor: 8 (over x, core).
Axes of the slice: x: 4, y: 4, z: 4, core: 2. Of those that a mesh axis runs over, the one named last changes fastest.
Arguments:
- tokens: bfloat16 [1024, 8192], P('adapter', 'tensor'), may hold values from -6 to 6
- token_adapter: int32 [1024], P('adapter'), may hold values from 0 to 31, as said below
- adapter_slot_table: int32 [32], replicated, may hold values from 0 to 31, each once
- gate_matrix: bfloat16 [8192, 28672], P(None, ('adapter', 'tensor')), may hold values from -0.0625 to 0.0625
- up_matrix: bfloat16 [8192, 28672], P(None, ('adapter', 'tensor')), may hold values from -0.0625 to 0.0625
- down_matrix: bfloat16 [28672, 8192], P(('adapter', 'tensor')), may hold values from -0.03125 to 0.03125
- adapter_entry_maps: bfloat16 [32, 8192, 128], P('adapter'), may hold values from -0.0625 to 0.0625
- adapter_gate_exit: bfloat16 [32, 64, 28672], P(None, None, ('adapter', 'tensor')), may hold values from -0.375 to 0.375
- adapter_up_exit: bfloat16 [32, 64, 28672], P(None, None, ('adapter', 'tensor')), may hold values from -0.375 to 0.375
- adapter_down_entry: bfloat16 [32, 28672, 64], P(None, ('adapter', 'tensor')), may hold values from -0.03125 to 0.03125
- adapter_down_exit: bfloat16 [32, 64, 8192], P('adapter', None, 'tensor'), may hold values from -0.375 to 0.375
Outputs:
- mixed: bfloat16 [1024, 8192], P('adapter', 'tensor')
The draws below stay inside these ranges and needn't reach their ends.
Inputs may be any that keep to these rules, and one draw needn't show every extreme that they name: `token_adapter`: every adapter is the adapter of 1 to 80 tokens, and some adapter of exactly 80. `adapter_slot_table`: each slot number appears once.
All inputs are finite; a program needn't handle non-finite values.
Results may differ from the reference program's by a relative error of at most 0.0055.
Values may be sent and summed in bfloat16 or wider, within the bound.
No kernel may reach another device: no remote copies, remote signals or barrier semaphores. Data moves between devices by JAX's collectives and lax.ppermute only.
A program may use at most 192 MiB of HBM per device.

```python
import jax
import jax.numpy as jnp

MODEL_WIDTH = 8192
HIDDEN_UNITS = 28672
ADAPTER_RANK = 64
ADAPTER_TOTAL = 32
TOKENS = 1024
SEGMENT_TOKENS = 80


def draw_token_adapter(key, part):
    key = jax.random.fold_in(key, 11)
    key_weights, key_extra, key_which, key_shuffle = jax.random.split(key, 4)
    others = ADAPTER_TOTAL - 1
    weights = jax.random.randint(key_weights, (others,), 3, 7).astype(jnp.int32)
    spare = TOKENS - SEGMENT_TOKENS - others
    counts = 1 + spare * weights // jnp.sum(weights)
    leftover = TOKENS - SEGMENT_TOKENS - jnp.sum(counts)
    extra_order = jax.random.permutation(key_extra, others).astype(jnp.int32)
    counts = counts + (extra_order < leftover).astype(jnp.int32)
    lengths = jnp.concatenate([jnp.full((1,), SEGMENT_TOKENS, jnp.int32), counts.astype(jnp.int32)])
    which = jax.random.permutation(key_which, ADAPTER_TOTAL).astype(jnp.int32)
    ends = jnp.cumsum(lengths)
    position = jnp.arange(TOKENS, dtype=jnp.int32)
    segment = jnp.sum((position[:, None] >= ends[None, :]).astype(jnp.int32), axis=1)
    sorted_ids = which[segment]
    shuffle = jax.random.permutation(key_shuffle, TOKENS).astype(jnp.int32)
    return sorted_ids[shuffle].astype(jnp.int32)


def shard_levels(key, extent, cuts, smallest, largest):
    def one(axis_at, parts):
        steps = jax.random.uniform(jax.random.fold_in(jax.random.fold_in(key, 6), axis_at), (parts,), jnp.float32, smallest / len(cuts), largest / len(cuts))
        return jnp.repeat(jnp.exp(steps), extent[axis_at] // parts).reshape((-1,) + (1,) * (len(extent) - axis_at - 1))

    loudness = one(*cuts[0])
    for cut in cuts[1:]:
        loudness = loudness * one(*cut)
    return loudness


def bell_draw(own_key, shape, width, reach, cuts=(), held_as=jnp.bfloat16):
    values = jax.random.normal(own_key, shape, jnp.float32) * width
    if len(cuts) > 0:
        values = shard_levels(own_key, shape, cuts, -0.22, 0.18) * values
    return jnp.clip(values, min=-reach, max=reach).astype(held_as)


def setup_inputs(seed: int = 0) -> dict:
    streams_of = jax.random.split(jax.random.key(seed), 12)
    return {
        "tokens": bell_draw(streams_of[0], (TOKENS, MODEL_WIDTH), 1.0, 6.0, ((0, 16), (1, 8))),
        "token_adapter": draw_token_adapter(jax.random.fold_in(streams_of[11], 71), 0),
        "adapter_slot_table": jax.random.permutation(streams_of[2], ADAPTER_TOTAL).astype(jnp.int32),
        "gate_matrix": bell_draw(streams_of[3], (MODEL_WIDTH, HIDDEN_UNITS), MODEL_WIDTH ** -0.5, 0.0625, ((1, 128),)),
        "up_matrix": bell_draw(streams_of[4], (MODEL_WIDTH, HIDDEN_UNITS), MODEL_WIDTH ** -0.5, 0.0625, ((1, 128),)),
        "down_matrix": bell_draw(streams_of[5], (HIDDEN_UNITS, MODEL_WIDTH), HIDDEN_UNITS ** -0.5, 0.03125, ((0, 128),)),
        "adapter_entry_maps": bell_draw(streams_of[6], (ADAPTER_TOTAL, MODEL_WIDTH, 2 * ADAPTER_RANK), MODEL_WIDTH ** -0.5, 0.0625, ((0, 16),)),
        "adapter_gate_exit": bell_draw(streams_of[7], (ADAPTER_TOTAL, ADAPTER_RANK, HIDDEN_UNITS), (4 * ADAPTER_RANK) ** -0.5, 0.375, ((2, 128),)),
        "adapter_up_exit": bell_draw(streams_of[8], (ADAPTER_TOTAL, ADAPTER_RANK, HIDDEN_UNITS), (4 * ADAPTER_RANK) ** -0.5, 0.375, ((2, 128),)),
        "adapter_down_entry": bell_draw(streams_of[9], (ADAPTER_TOTAL, HIDDEN_UNITS, ADAPTER_RANK), HIDDEN_UNITS ** -0.5, 0.03125, ((1, 128),)),
        "adapter_down_exit": bell_draw(streams_of[10], (ADAPTER_TOTAL, ADAPTER_RANK, MODEL_WIDTH), (4 * ADAPTER_RANK) ** -0.5, 0.375, ((0, 16), (2, 8))),
    }


def token_layout(token_adapter, adapter_slot_table, seg_rows):
    token_count = token_adapter.shape[0]
    adapter_count = adapter_slot_table.shape[0]
    member = (token_adapter[:, None] == jnp.arange(adapter_count, dtype=jnp.int32)[None, :]).astype(jnp.int32)
    earlier = jnp.cumsum(member, axis=0) - member
    rank_in = jnp.sum(earlier * member, axis=1)
    slot_index = jnp.sum(member * adapter_slot_table[None, :], axis=1)
    slot_row = (slot_index * seg_rows + rank_in).astype(jnp.int32)
    token_of_row = jnp.full((adapter_count * seg_rows,), token_count, jnp.int32)
    token_of_row = token_of_row.at[slot_row].set(jnp.arange(token_count, dtype=jnp.int32))
    return slot_row, token_of_row


def reference(tokens, token_adapter, adapter_slot_table, gate_matrix, up_matrix, down_matrix, adapter_entry_maps, adapter_gate_exit, adapter_up_exit, adapter_down_entry, adapter_down_exit):
    slot_row, token_of_row = token_layout(token_adapter, adapter_slot_table, SEGMENT_TOKENS)
    is_filled = token_of_row < TOKENS
    safe_index = jnp.minimum(token_of_row, TOKENS - 1)
    padded_input = jnp.where(is_filled[:, None], tokens[safe_index], 0).reshape(ADAPTER_TOTAL, SEGMENT_TOKENS, MODEL_WIDTH)
    reduced_gate_up = jnp.einsum("ace,aeg->acg", padded_input.astype(jnp.float32), adapter_entry_maps.astype(jnp.float32)).astype(jnp.bfloat16)
    reduced_single = reduced_gate_up.astype(jnp.float32)
    gate_correction = jnp.einsum("mdq,mqn->mdn", reduced_single[..., :ADAPTER_RANK], adapter_gate_exit.astype(jnp.float32)).reshape(ADAPTER_TOTAL * SEGMENT_TOKENS, HIDDEN_UNITS)
    gate_sum = jnp.dot(tokens, gate_matrix, preferred_element_type=jnp.float32) + gate_correction[slot_row]
    up_correction = jnp.einsum("mdq,mqn->mdn", reduced_single[..., ADAPTER_RANK:], adapter_up_exit.astype(jnp.float32)).reshape(ADAPTER_TOTAL * SEGMENT_TOKENS, HIDDEN_UNITS)
    up_sum = jnp.dot(tokens, up_matrix, preferred_element_type=jnp.float32) + up_correction[slot_row]
    hidden = (jax.nn.silu(gate_sum) * up_sum).astype(jnp.bfloat16)
    hidden_padded = jnp.where(is_filled[:, None], hidden[safe_index], 0).reshape(ADAPTER_TOTAL, SEGMENT_TOKENS, HIDDEN_UNITS)
    reduced_down = jnp.einsum("uvm,umj->uvj", hidden_padded.astype(jnp.float32), adapter_down_entry.astype(jnp.float32)).astype(jnp.bfloat16)
    down_correction = jnp.einsum("uhz,uza->uha", reduced_down.astype(jnp.float32), adapter_down_exit.astype(jnp.float32)).reshape(ADAPTER_TOTAL * SEGMENT_TOKENS, MODEL_WIDTH)
    mixed = jnp.dot(hidden, down_matrix, preferred_element_type=jnp.float32) + down_correction[slot_row]
    return mixed.astype(jnp.bfloat16)
```

```python
import functools

import jax
import jax.numpy as jnp
import numpy as np
from jax import lax
from jax.experimental import pallas as pl
from jax.experimental.pallas import tpu as pltpu
from jax.sharding import PartitionSpec as P

SEGMENT = 80
BF = jnp.bfloat16
F32 = jnp.float32
AXES = ("adapter", "tensor")
VMEM_LIMIT = 60 * 1024 * 1024


def pairs(move):
    out = []
    for i in range(128):
        y, z, x, c = i // 32, (i // 8) % 4, (i // 2) % 4, i % 2
        ty, tz, tx, tc = move(y, z, x, c)
        out.append((i, (ty % 4) * 32 + (tz % 4) * 8 + (tx % 4) * 2 + tc % 2))
    return out


def send(value, dy=0, dz=0, dx=0, dc=0):
    return lax.ppermute(value, AXES, pairs(lambda y, z, x, c: (y + dy, z + dz, x + dx, c + dc)))


def ring(value, axis):
    def move(y, z, x, c):
        d = 1 - 2 * c
        return (y + d, z, x, c) if axis == "y" else (y, z + d, x, c)

    return lax.ppermute(value, AXES, pairs(move))


def params(n=1):
    return pltpu.CompilerParams(
        dimension_semantics=("arbitrary",) * n, vmem_limit_bytes=VMEM_LIMIT
    )


def low_kernel(x_ref, e_ref, s_ref, o_ref, acc):
    k = pl.program_id(0)
    x = x_ref[...].reshape(1024, 1024)

    @pl.when(k == 0)
    def _():
        acc[...] = jnp.zeros_like(acc)

    for j in range(2):
        acc[j] += jnp.dot(x, e_ref[j], preferred_element_type=F32)

    @pl.when(k == pl.num_programs(0) - 1)
    def _():
        for j in range(2):
            o_ref[j] = jnp.dot(
                s_ref[j], acc[j].astype(BF), preferred_element_type=F32
            ).astype(BF)


def low_own_rows(every, entry, select):
    return pl.pallas_call(
        low_kernel,
        grid=(8,),
        in_specs=[
            pl.BlockSpec((16, 1, 64, 1024), lambda k: (0, k, 0, 0)),
            pl.BlockSpec((2, 1024, 128), lambda k: (0, k, 0)),
            pl.BlockSpec((2, SEGMENT, 1024), lambda k: (0, 0, 0)),
        ],
        out_specs=pl.BlockSpec((2, SEGMENT, 128), lambda k: (0, 0, 0)),
        out_shape=jax.ShapeDtypeStruct((2, SEGMENT, 128), BF),
        scratch_shapes=[pltpu.VMEM((2, 1024, 128), F32)],
        compiler_params=params(),
        cost_estimate=pl.CostEstimate(
            flops=2 * 1024 * 8192 * 256, bytes_accessed=21 << 20, transcendentals=0
        ),
        name="low_own",
    )(every, entry, select)


def gate_up_kernel(x_ref, g_ref, u_ref, go_ref, uo_ref):
    k = pl.program_id(0)
    x = x_ref[...].reshape(1024, 1024)

    @pl.when(k == 0)
    def _():
        go_ref[...] = jnp.zeros_like(go_ref)
        uo_ref[...] = jnp.zeros_like(uo_ref)

    go_ref[...] += jnp.dot(x, g_ref[...], preferred_element_type=F32)
    uo_ref[...] += jnp.dot(x, u_ref[...], preferred_element_type=F32)


def gate_up(every, gate, up):
    n = gate.shape[1]
    return pl.pallas_call(
        gate_up_kernel,
        grid=(8,),
        in_specs=[
            pl.BlockSpec((16, 1, 64, 1024), lambda k: (0, k, 0, 0)),
            pl.BlockSpec((1024, n), lambda k: (k, 0)),
            pl.BlockSpec((1024, n), lambda k: (k, 0)),
        ],
        out_specs=[pl.BlockSpec((1024, n), lambda k: (0, 0))] * 2,
        out_shape=[jax.ShapeDtypeStruct((1024, n), F32)] * 2,
        compiler_params=params(),
        cost_estimate=pl.CostEstimate(
            flops=2 * 1024 * 8192 * 512, bytes_accessed=25 << 20, transcendentals=0
        ),
        name="gate_up",
    )(every, gate, up)


def hidden_kernel(
    place, g_ref, u_ref, q_ref, m_ref, low_ref, ge_ref, ue_ref, de_ref, h_ref, d_ref
):
    low = jnp.dot(q_ref[...], low_ref[...], preferred_element_type=F32)
    lg = low[:, :64].astype(BF)
    lu = low[:, 64:].astype(BF)
    lg = jnp.concatenate([lg] * 4, axis=1)
    lu = jnp.concatenate([lu] * 4, axis=1)
    gate = g_ref[...]
    up = u_ref[...]
    for j in range(8):
        mask = m_ref[:, 256 * j : 256 * (j + 1)]
        gate += jnp.dot(lg * mask, ge_ref[pl.ds(256 * j, 256)], preferred_element_type=F32)
        up += jnp.dot(lu * mask, ue_ref[pl.ds(256 * j, 256)], preferred_element_type=F32)
    hidden = (gate / (1.0 + jnp.exp(-gate)) * up).astype(BF)
    down = jnp.zeros((256, 256), F32)
    for j in range(8):
        mask = m_ref[:, 256 * j : 256 * (j + 1)].astype(F32)
        down += jnp.dot(hidden, de_ref[j], preferred_element_type=F32) * mask
    down = down[:, :128] + down[:, 128:]
    for z in range(4):
        at = place[4 + z]
        h_ref[0, at] = hidden[64 * z : 64 * (z + 1)]
        d_ref[0, at] = down[64 * z : 64 * (z + 1)]


def hidden_rows(place, gate, up, pick, mask, low, gate_exit, up_exit, down_entry):
    n = gate.shape[1]
    return pl.pallas_call(
        hidden_kernel,
        grid_spec=pltpu.PrefetchScalarGridSpec(
            num_scalar_prefetch=1,
            grid=(4,),
            in_specs=[
                pl.BlockSpec((256, n), lambda i, p: (i, 0)),
                pl.BlockSpec((256, n), lambda i, p: (i, 0)),
                pl.BlockSpec((256, 2560), lambda i, p: (i, 0)),
                pl.BlockSpec((256, 2048), lambda i, p: (i, 0)),
                pl.BlockSpec((2560, 128), lambda i, p: (0, 0)),
                pl.BlockSpec((2048, n), lambda i, p: (0, 0)),
                pl.BlockSpec((2048, n), lambda i, p: (0, 0)),
                pl.BlockSpec((8, n, 256), lambda i, p: (0, 0, 0)),
            ],
            out_specs=[
                pl.BlockSpec((1, 4, 64, n), lambda i, p: (p[i], 0, 0, 0)),
                pl.BlockSpec((1, 4, 64, 128), lambda i, p: (p[i], 0, 0, 0)),
            ],
        ),
        out_shape=[
            jax.ShapeDtypeStruct((4, 4, 64, n), BF),
            jax.ShapeDtypeStruct((4, 4, 64, 128), F32),
        ],
        compiler_params=params(),
        cost_estimate=pl.CostEstimate(
            flops=2 * 1024 * 2560 * 512, bytes_accessed=16 << 20, transcendentals=1024 * n
        ),
        name="hidden_rows",
    )(place, gate, up, pick, mask, low, gate_exit, up_exit, down_entry)


def part_kernel(with_ring, with_extra, *refs):
    refs = list(refs)
    h_ref, w_ref, c_ref = refs[:3]
    o_ref = refs[-1]
    rest = refs[3:-1]
    r_ref = rest.pop(0) if with_ring else None
    n = w_ref.shape[1]
    for j in range(0, n, 1024):
        at = pl.ds(j, 1024)
        total = jnp.dot(h_ref[...], w_ref[:, at], preferred_element_type=F32)
        total += c_ref[:, at].astype(F32)
        if with_ring:
            total += r_ref[:, at].astype(F32)
        o_ref[:, at] = total.astype(o_ref.dtype)
    if with_extra:
        d_ref, e_ref = rest
        total = d_ref[...] + e_ref[...].astype(F32)
        if with_ring:
            total += r_ref[:, pl.ds(n, 128)].astype(F32)
        o_ref[:, pl.ds(n, 128)] = total.astype(o_ref.dtype)


def part(h, w, other, row, column, ringed, extra, dtype):
    rows, k = h.shape
    n = w.shape[1]
    args = [h, w, other]
    specs = [
        pl.BlockSpec((rows, k), lambda i: (0, 0)),
        pl.BlockSpec((k, n), lambda i: (0, 0)),
        pl.BlockSpec((rows, n), lambda i: (row, column)),
    ]
    if ringed is not None:
        args.append(ringed)
        specs.append(pl.BlockSpec(ringed.shape, lambda i: (0, 0)))
    if extra is not None:
        for e in extra:
            args.append(e)
            specs.append(pl.BlockSpec(e.shape, lambda i: (0, 0)))
    width = n + (128 if extra is not None else 0)
    return pl.pallas_call(
        functools.partial(part_kernel, ringed is not None, extra is not None),
        grid=(1,),
        in_specs=specs,
        out_specs=pl.BlockSpec((rows, width), lambda i: (0, 0)),
        out_shape=jax.ShapeDtypeStruct((rows, width), dtype),
        compiler_params=params(),
        cost_estimate=pl.CostEstimate(
            flops=2 * rows * 256 * n, bytes_accessed=2 * n * (k + 3 * rows), transcendentals=0
        ),
        name="part",
    )(*args)


def on_device(
    tokens,
    token_adapter,
    adapter_slot_table,
    gate_matrix,
    up_matrix,
    down_matrix,
    adapter_entry_maps,
    adapter_gate_exit,
    adapter_up_exit,
    adapter_down_entry,
    adapter_down_exit,
):
    units = gate_matrix.shape[1]
    a = lax.axis_index("adapter")
    t = lax.axis_index("tensor")
    y, z, x, c = a // 4, a % 4, t // 2, t % 2
    way = 1 - 2 * c

    every = lax.all_gather(tokens, AXES, axis=0, tiled=False).reshape(16, 8, 64, 1024)
    ids = lax.all_gather(token_adapter, "adapter", axis=0, tiled=True)

    names = jnp.arange(32, dtype=jnp.int32)
    member = ids[:, None] == names[None, :]
    order = jnp.arange(1024, dtype=jnp.int32)
    before = (order[:, None] > order[None, :]).astype(BF)
    earlier = jnp.dot(before, member.astype(BF), preferred_element_type=F32).astype(jnp.int32)
    rank_in = jnp.sum(jnp.where(member, earlier, 0), axis=1)
    slot = jnp.sum(jnp.where(member, adapter_slot_table[None, :], 0), axis=1)
    owner = slot // 2
    row = (slot % 2) * SEGMENT + rank_in
    select = (
        (jnp.where(owner == a, row, -1))[None, :] == jnp.arange(160, dtype=jnp.int32)[:, None]
    ).astype(BF).reshape(2, SEGMENT, 1024)
    relative = ((owner % 4 - z) % 4) * 4 + (owner // 4 - y) % 4
    pick = (
        (relative * 160 + row)[:, None] == jnp.arange(2560, dtype=jnp.int32)[None, :]
    ).astype(BF)
    mask = (slot[:, None] == (jnp.arange(2048, dtype=jnp.int32) // 64)[None, :]).astype(BF)

    def column(r, core):
        at = ((x + r) % 4 * 2 + core) * 1024
        return lax.dynamic_slice(down_matrix, (0, at), (units, 1024))

    chunks = ((1, 2), (3, 0))
    mine = [jnp.concatenate([column(r, c) for r in ch], axis=1) for ch in chunks]
    theirs = jnp.concatenate([column(r, 1 - c) for ch in chunks for r in ch], axis=1)
    entry_four = (
        adapter_down_entry.reshape(8, 4, units, 64).transpose(0, 2, 1, 3).reshape(8, units, 256)
    )

    low_own = low_own_rows(every, adapter_entry_maps, select).reshape(160, 128)
    low = jnp.stack([low_own] + [send(low_own, dy=-d) for d in (1, 2, 3)])
    low = jnp.stack([low] + [send(low, dz=-d) for d in (1, 2, 3)]).reshape(2560, 128)
    gate, up = gate_up(every, gate_matrix, up_matrix)

    exit_in, _ = lax.optimization_barrier((adapter_down_exit, low_own))
    exits = lax.all_gather(exit_in, "adapter", axis=0, tiled=True).reshape(2048, 1024)

    quarter = jnp.arange(4, dtype=jnp.int32)
    place = jnp.concatenate([way * (y - quarter) % 4, way * (z - quarter) % 4])
    hidden, extra = hidden_rows(
        place,
        gate,
        up,
        pick,
        mask,
        low,
        adapter_gate_exit.reshape(2048, units),
        adapter_up_exit.reshape(2048, units),
        entry_four,
    )
    back = np.array([0, 3, 2, 1])

    def block(v, color, r):
        v = v[:, r, :32] if color == 0 else v[r, :, 32:]
        return v.reshape(128, v.shape[-1])

    def back_block(v, color, r):
        r = int(back[r])
        v = v[:, r, :32] if color == 0 else v[r, :, 32:]
        v = jnp.stack([v[int(b)] for b in back])
        return v.reshape(128, v.shape[-1])

    turn = (1, 2, 3, 0)
    other = {}
    for r in turn:
        rows = jnp.concatenate([back_block(hidden, 0, r), back_block(hidden, 1, r)])
        product = jnp.dot(rows, theirs, preferred_element_type=F32).astype(BF)
        other[r] = send(product, dc=1)
    theirs_extra = send(
        jnp.stack([jnp.stack([back_block(extra, k, r) for r in range(4)]) for k in range(2)]).astype(BF),
        dc=1,
    )

    axes = (("z", "y"), ("y", "z"))
    state = {}
    for r in turn:
        for ch in range(2):
            for color in range(2):
                ringed = None if r == 1 else ring(state[ch, color], axes[color][0])
                own_extra = (
                    (block(extra, color, r), theirs_extra[color, r]) if ch == 1 else None
                )
                state[ch, color] = part(
                    block(hidden, color, r),
                    mine[ch],
                    other[r],
                    color,
                    ch,
                    ringed,
                    own_extra,
                    F32 if r == 0 else BF,
                )
    for ch in range(2):
        for color in range(2):
            held = state[ch, color].reshape(4, 32, -1)
            running = held[1]
            for r in (2, 3, 0):
                running = held[r] + ring(running.astype(BF), axes[color][1]).astype(F32)
            state[ch, color] = running
    summed = [jnp.concatenate([state[ch, 0], state[ch, 1]]) for ch in range(2)]
    tail = summed[1][:, 2048:]
    blocks = {
        1: summed[0][:, :1024],
        2: summed[0][:, 1024:],
        3: summed[1][:, :1024],
        0: summed[1][:, 1024:2048],
    }
    total = jnp.concatenate([blocks[0], tail], axis=1)
    for r in (1, 2, 3):
        total = total + send(
            jnp.concatenate([blocks[r], tail], axis=1).astype(BF), dx=r
        ).astype(F32)

    own_slot = jnp.sum(
        jnp.where(token_adapter[:, None] == names[None, :], adapter_slot_table[None, :], 0), axis=1
    )
    low_down = total[:, 1024:].astype(BF)
    spread = jnp.tile(low_down, (1, 16))
    spread = jnp.where(
        (own_slot // 2)[:, None] == (jnp.arange(2048, dtype=jnp.int32) // 128)[None, :], spread, 0
    )
    delta = jnp.dot(spread, exits, preferred_element_type=F32)
    return (total[:, :1024] + delta).astype(BF)


def solution(mesh):
    return jax.shard_map(
        on_device,
        mesh=mesh,
        in_specs=(
            P("adapter", "tensor"),
            P("adapter"),
            P(),
            P(None, ("adapter", "tensor")),
            P(None, ("adapter", "tensor")),
            P(("adapter", "tensor"), None),
            P("adapter", None, None),
            P(None, None, ("adapter", "tensor")),
            P(None, None, ("adapter", "tensor")),
            P(None, ("adapter", "tensor"), None),
            P("adapter", None, "tensor"),
        ),
        out_specs=P("adapter", "tensor"),
        check_vma=False,
    )
```

```python
import functools

import jax
import jax.numpy as jnp
from jax import lax
from jax.experimental import pallas as pl
from jax.experimental.pallas import tpu as pltpu
from jax.sharding import PartitionSpec as P

SEGMENT = 80
BF = jnp.bfloat16
F32 = jnp.float32
AXES = ("adapter", "tensor")
VMEM_LIMIT = 60 * 1024 * 1024


def pairs(move):
    out = []
    for i in range(128):
        y, z, x, c = i // 32, (i // 8) % 4, (i // 2) % 4, i % 2
        ty, tz, tx, tc = move(y, z, x, c)
        out.append((i, (ty % 4) * 32 + (tz % 4) * 8 + (tx % 4) * 2 + tc % 2))
    return out


def send(value, dy=0, dz=0, dx=0, dc=0):
    return lax.ppermute(value, AXES, pairs(lambda y, z, x, c: (y + dy, z + dz, x + dx, c + dc)))


def ring(value, axis):
    def move(y, z, x, c):
        d = 1 - 2 * c
        return (y + d, z, x, c) if axis == "y" else (y, z + d, x, c)

    return lax.ppermute(value, AXES, pairs(move))


def params(n=1):
    return pltpu.CompilerParams(
        dimension_semantics=("arbitrary",) * n, vmem_limit_bytes=VMEM_LIMIT
    )


def nt(a, b):
    return lax.dot_general(a, b, (((1,), (1,)), ((), ())), preferred_element_type=F32)


def low_kernel(x_ref, e_ref, s_ref, o_ref, acc):
    k = pl.program_id(0)

    @pl.when(k == 0)
    def _():
        acc[...] = jnp.zeros_like(acc)

    for j in range(2):
        x = x_ref[:, j].reshape(1024, 1024)
        at = pl.ds(1024 * j, 1024)
        e = jnp.concatenate([e_ref[0, at], e_ref[1, at]], axis=1)
        acc[...] += jnp.dot(x, e, preferred_element_type=F32)

    @pl.when(k == pl.num_programs(0) - 1)
    def _():
        for j in range(2):
            o_ref[j] = jnp.dot(
                s_ref[j], acc[:, 128 * j : 128 * (j + 1)].astype(BF), preferred_element_type=F32
            ).astype(BF)


def low_own_rows(every, entry, select):
    return pl.pallas_call(
        low_kernel,
        grid=(4,),
        in_specs=[
            pl.BlockSpec((16, 2, 64, 1024), lambda k: (0, k, 0, 0)),
            pl.BlockSpec((2, 2048, 128), lambda k: (0, k, 0)),
            pl.BlockSpec((2, SEGMENT, 1024), lambda k: (0, 0, 0)),
        ],
        out_specs=pl.BlockSpec((2, SEGMENT, 128), lambda k: (0, 0, 0)),
        out_shape=jax.ShapeDtypeStruct((2, SEGMENT, 128), BF),
        scratch_shapes=[pltpu.VMEM((1024, 256), F32)],
        compiler_params=params(),
        cost_estimate=pl.CostEstimate(
            flops=2 * 1024 * 8192 * 256, bytes_accessed=21 << 20, transcendentals=0
        ),
        name="low_own",
    )(every, entry, select)


def gate_up_kernel(x_ref, g_ref, u_ref, go_ref, uo_ref):
    k = pl.program_id(0)

    @pl.when(k == 0)
    def _():
        go_ref[...] = jnp.zeros_like(go_ref)
        uo_ref[...] = jnp.zeros_like(uo_ref)

    for j in range(2):
        x = x_ref[:, j].reshape(1024, 1024)
        at = pl.ds(1024 * j, 1024)
        go_ref[...] += nt(x, g_ref[:, at])
        uo_ref[...] += nt(x, u_ref[:, at])


def gate_up(every, gate, up):
    n = gate.shape[0]
    return pl.pallas_call(
        gate_up_kernel,
        grid=(4,),
        in_specs=[
            pl.BlockSpec((16, 2, 64, 1024), lambda k: (0, k, 0, 0)),
            pl.BlockSpec((n, 2048), lambda k: (0, k)),
            pl.BlockSpec((n, 2048), lambda k: (0, k)),
        ],
        out_specs=[pl.BlockSpec((1024, n), lambda k: (0, 0))] * 2,
        out_shape=[jax.ShapeDtypeStruct((1024, n), F32)] * 2,
        compiler_params=params(),
        cost_estimate=pl.CostEstimate(
            flops=2 * 1024 * 8192 * 512, bytes_accessed=25 << 20, transcendentals=0
        ),
        name="gate_up",
    )(every, gate, up)


def hidden_kernel(
    place, g_ref, u_ref, q_ref, m_ref, low_ref, ge_ref, ue_ref, de_ref, ha_ref, hb_ref, da_ref, db_ref
):
    low = jnp.dot(q_ref[...], low_ref[...], preferred_element_type=F32)
    lg = low[:, :64].astype(BF)
    lu = low[:, 64:].astype(BF)
    lg = jnp.concatenate([lg] * 4, axis=1)
    lu = jnp.concatenate([lu] * 4, axis=1)
    gate = g_ref[...]
    up = u_ref[...]
    for j in range(8):
        mask = m_ref[:, 256 * j : 256 * (j + 1)]
        gate += jnp.dot(lg * mask, ge_ref[pl.ds(256 * j, 256)], preferred_element_type=F32)
        up += jnp.dot(lu * mask, ue_ref[pl.ds(256 * j, 256)], preferred_element_type=F32)
    hidden = (gate / (1.0 + jnp.exp(-gate)) * up).astype(BF)
    down = jnp.zeros((256, 256), F32)
    for j in range(8):
        mask = m_ref[:, 256 * j : 256 * (j + 1)].astype(F32)
        down += nt(hidden, de_ref[pl.ds(256 * j, 256)]) * mask
    down = down[:, :128] + down[:, 128:]
    for z in range(4):
        at = place[4 + z]
        ha_ref[at, 0] = hidden[64 * z : 64 * z + 32]
        hb_ref[0, at] = hidden[64 * z + 32 : 64 * z + 64]
        da_ref[at, 0] = down[64 * z : 64 * z + 32]
        db_ref[0, at] = down[64 * z + 32 : 64 * z + 64]


def hidden_rows(place, gate, up, pick, mask, low, gate_exit, up_exit, down_entry):
    n = gate.shape[1]
    return pl.pallas_call(
        hidden_kernel,
        grid_spec=pltpu.PrefetchScalarGridSpec(
            num_scalar_prefetch=1,
            grid=(4,),
            in_specs=[
                pl.BlockSpec((256, n), lambda i, p: (i, 0)),
                pl.BlockSpec((256, n), lambda i, p: (i, 0)),
                pl.BlockSpec((256, 2560), lambda i, p: (i, 0)),
                pl.BlockSpec((256, 2048), lambda i, p: (i, 0)),
                pl.BlockSpec((2560, 128), lambda i, p: (0, 0)),
                pl.BlockSpec((2048, n), lambda i, p: (0, 0)),
                pl.BlockSpec((2048, n), lambda i, p: (0, 0)),
                pl.BlockSpec((2048, n), lambda i, p: (0, 0)),
            ],
            out_specs=[
                pl.BlockSpec((4, 1, 32, n), lambda i, p: (0, p[i], 0, 0)),
                pl.BlockSpec((1, 4, 32, n), lambda i, p: (p[i], 0, 0, 0)),
                pl.BlockSpec((4, 1, 32, 128), lambda i, p: (0, p[i], 0, 0)),
                pl.BlockSpec((1, 4, 32, 128), lambda i, p: (p[i], 0, 0, 0)),
            ],
        ),
        out_shape=[jax.ShapeDtypeStruct((4, 4, 32, n), BF)] * 2
        + [jax.ShapeDtypeStruct((4, 4, 32, 128), F32)] * 2,
        compiler_params=params(),
        cost_estimate=pl.CostEstimate(
            flops=2 * 1024 * 2560 * 512, bytes_accessed=16 << 20, transcendentals=1024 * n
        ),
        name="hidden_rows",
    )(place, gate, up, pick, mask, low, gate_exit, up_exit, down_entry)


WIDE = 4096 + 128
TILE = WIDE // 3


def turned(v):
    return jnp.concatenate([v[0, g] for g in (0, 3, 2, 1)], axis=0)


def straight(v):
    return v[0].reshape(128, v.shape[-1])


def part_kernel(arrange, with_other, ha_ref, hb_ref, da_ref, db_ref, w_ref, *refs):
    o_ref = refs[-1]
    rows = jnp.concatenate([arrange(ha_ref[...]), arrange(hb_ref[...])], axis=0)
    total = jnp.dot(rows, w_ref[...], preferred_element_type=F32).reshape(2, 128, TILE)
    if with_other:
        total += refs[0][0].astype(F32)
    o_ref[0] = total.astype(o_ref.dtype)

    @pl.when(pl.program_id(0) == 2)
    def _():
        extra = jnp.concatenate([arrange(da_ref[...]), arrange(db_ref[...])], axis=0)
        extra = extra.reshape(2, 128, 128)
        o_ref[0, :, :, TILE - 128 :] = (total[:, :, TILE - 128 :] + extra).astype(o_ref.dtype)


def part(ha, hb, da, db, w, other, first, count, back, dtype):
    n = ha.shape[-1]

    def at(t, i):
        r = (first + i) % 4
        return ((4 - r) % 4 if back else r), 0, 0, 0

    args = [ha, hb, da, db, w]
    specs = [
        pl.BlockSpec((1, 4, 32, n), at),
        pl.BlockSpec((1, 4, 32, n), at),
        pl.BlockSpec((1, 4, 32, 128), at),
        pl.BlockSpec((1, 4, 32, 128), at),
        pl.BlockSpec((n, TILE), lambda t, i: (0, t)),
    ]
    if other is not None:
        args.append(other)
        specs.append(pl.BlockSpec((1, 2, 128, TILE), lambda t, i: (i, 0, 0, t)))
    return pl.pallas_call(
        functools.partial(part_kernel, turned if back else straight, other is not None),
        grid=(3, count),
        in_specs=specs,
        out_specs=pl.BlockSpec((1, 2, 128, TILE), lambda t, i: (i, 0, 0, t)),
        out_shape=jax.ShapeDtypeStruct((count, 2, 128, WIDE), dtype),
        compiler_params=params(2),
        cost_estimate=pl.CostEstimate(
            flops=2 * 256 * 256 * WIDE * count,
            bytes_accessed=WIDE * 2 * (224 + 256 * count * 3),
            transcendentals=0,
        ),
        name="part",
    )(*args)


def on_device(
    tokens,
    token_adapter,
    adapter_slot_table,
    gate_matrix,
    up_matrix,
    down_matrix,
    adapter_entry_maps,
    adapter_gate_exit,
    adapter_up_exit,
    adapter_down_entry,
    adapter_down_exit,
):
    units = gate_matrix.shape[1]
    a = lax.axis_index("adapter")
    t = lax.axis_index("tensor")
    y, z, x, c = a // 4, a % 4, t // 2, t % 2
    way = 1 - 2 * c

    every = lax.all_gather(tokens, AXES, axis=0, tiled=False).reshape(16, 8, 64, 1024)
    ids = lax.all_gather(token_adapter, "adapter", axis=0, tiled=True)

    names = jnp.arange(32, dtype=jnp.int32)
    member = ids[:, None] == names[None, :]
    order = jnp.arange(1024, dtype=jnp.int32)
    before = (order[:, None] > order[None, :]).astype(BF)
    earlier = jnp.dot(before, member.astype(BF), preferred_element_type=F32).astype(jnp.int32)
    rank_in = jnp.sum(jnp.where(member, earlier, 0), axis=1)
    slot = jnp.sum(jnp.where(member, adapter_slot_table[None, :], 0), axis=1)
    owner = slot // 2
    row = (slot % 2) * SEGMENT + rank_in
    select = (
        (jnp.where(owner == a, row, -1))[None, :] == jnp.arange(160, dtype=jnp.int32)[:, None]
    ).astype(BF).reshape(2, SEGMENT, 1024)
    relative = ((owner % 4 - z) % 4) * 4 + (owner // 4 - y) % 4
    pick = (
        (relative * 160 + row)[:, None] == jnp.arange(2560, dtype=jnp.int32)[None, :]
    ).astype(BF)
    mask = (slot[:, None] == (jnp.arange(2048, dtype=jnp.int32) // 64)[None, :]).astype(BF)

    def column(r, core):
        at = ((x + r) % 4 * 2 + core) * 1024
        return lax.dynamic_slice(down_matrix, (0, at), (units, 1024))

    turns = (1, 2, 3, 0)
    empty = jnp.zeros((units, 128), BF)
    mine = jnp.concatenate([column(r, c) for r in turns] + [empty], axis=1)
    theirs = jnp.concatenate([column(r, 1 - c) for r in turns] + [empty], axis=1)

    low_own = low_own_rows(every, adapter_entry_maps, select).reshape(160, 128)
    low = jnp.stack([low_own] + [send(low_own, dy=-d) for d in (1, 2, 3)])
    low = jnp.stack([low] + [send(low, dz=-d) for d in (1, 2, 3)]).reshape(2560, 128)
    gate, up = gate_up(every, gate_matrix.T, up_matrix.T)

    exit_in, _ = lax.optimization_barrier((adapter_down_exit, low_own))
    exits = lax.all_gather(exit_in, "adapter", axis=0, tiled=True).reshape(2048, 1024)

    quarter = jnp.arange(4, dtype=jnp.int32)
    place = jnp.concatenate([way * (y - quarter) % 4, way * (z - quarter) % 4])
    rows = hidden_rows(
        place,
        gate,
        up,
        pick,
        mask,
        low,
        adapter_gate_exit.reshape(2048, units),
        adapter_up_exit.reshape(2048, units),
        adapter_down_entry.transpose(0, 2, 1).reshape(2048, units),
    )
    first_other = send(part(*rows, theirs, None, 1, 1, True, BF), dc=1)
    rest_other = send(part(*rows, theirs, None, 2, 3, True, BF), dc=1)
    first = part(*rows, mine, first_other, 1, 1, False, BF)
    rest = part(*rows, mine, rest_other, 2, 3, False, F32)

    axes = (("z", "y"), ("y", "z"))
    spans = ((0, 2048), (2048, WIDE))
    state = {}
    for step in range(3):
        for ch, (lo, hi) in enumerate(spans):
            for color in range(2):
                held = first[0, color, :, lo:hi] if step == 0 else state[ch, color]
                came = ring(held, axes[color][0]).astype(F32)
                own = rest[step, color, :, lo:hi]
                if step < 2:
                    state[ch, color] = (own + came).astype(BF)
                else:
                    state[ch, color] = (own.reshape(4, 32, -1), came.reshape(4, 32, -1))
    for ch in range(2):
        for color in range(2):
            own, came = state[ch, color]
            running = own[1] + came[1]
            for r in (2, 3, 0):
                running = own[r] + came[r] + ring(running.astype(BF), axes[color][1]).astype(F32)
            state[ch, color] = running
    summed = [jnp.concatenate([state[ch, 0], state[ch, 1]]) for ch in range(2)]
    tail = summed[1][:, 2048:]
    blocks = {
        1: summed[0][:, :1024],
        2: summed[0][:, 1024:],
        3: summed[1][:, :1024],
        0: summed[1][:, 1024:2048],
    }
    total = jnp.concatenate([blocks[0], tail], axis=1)
    for r in (1, 2, 3):
        total = total + send(
            jnp.concatenate([blocks[r], tail], axis=1).astype(BF), dx=r
        ).astype(F32)

    own_slot = jnp.sum(
        jnp.where(token_adapter[:, None] == names[None, :], adapter_slot_table[None, :], 0), axis=1
    )
    low_down = total[:, 1024:].astype(BF)
    spread = jnp.tile(low_down, (1, 16))
    spread = jnp.where(
        (own_slot // 2)[:, None] == (jnp.arange(2048, dtype=jnp.int32) // 128)[None, :], spread, 0
    )
    delta = jnp.dot(spread, exits, preferred_element_type=F32)
    return (total[:, :1024] + delta).astype(BF)


def solution(mesh):
    return jax.shard_map(
        on_device,
        mesh=mesh,
        in_specs=(
            P("adapter", "tensor"),
            P("adapter"),
            P(),
            P(None, ("adapter", "tensor")),
            P(None, ("adapter", "tensor")),
            P(("adapter", "tensor"), None),
            P("adapter", None, None),
            P(None, None, ("adapter", "tensor")),
            P(None, None, ("adapter", "tensor")),
            P(None, ("adapter", "tensor"), None),
            P("adapter", None, "tensor"),
        ),
        out_specs=P("adapter", "tensor"),
        check_vma=False,
    )
```

```python
import functools

import jax
import jax.numpy as jnp
from jax import lax
from jax.experimental import pallas as pl
from jax.experimental.pallas import tpu as pltpu
from jax.sharding import PartitionSpec as P

SEGMENT = 80
BF = jnp.bfloat16
F32 = jnp.float32
AXES = ("adapter", "tensor")
VMEM_LIMIT = 60 * 1024 * 1024


def pairs(move):
    out = []
    for i in range(128):
        y, z, x, c = i // 32, (i // 8) % 4, (i // 2) % 4, i % 2
        ty, tz, tx, tc = move(y, z, x, c)
        out.append((i, (ty % 4) * 32 + (tz % 4) * 8 + (tx % 4) * 2 + tc % 2))
    return out


def send(value, dy=0, dz=0, dx=0, dc=0):
    return lax.ppermute(value, AXES, pairs(lambda y, z, x, c: (y + dy, z + dz, x + dx, c + dc)))


def ring(value, axis):
    def move(y, z, x, c):
        d = 1 - 2 * c
        return (y + d, z, x, c) if axis == "y" else (y, z + d, x, c)

    return lax.ppermute(value, AXES, pairs(move))


def params(n=1):
    return pltpu.CompilerParams(
        dimension_semantics=("arbitrary",) * n, vmem_limit_bytes=VMEM_LIMIT
    )


def nt(a, b):
    return lax.dot_general(a, b, (((1,), (1,)), ((), ())), preferred_element_type=F32)


def low_kernel(x_ref, e_ref, s_ref, o_ref, acc):
    k = pl.program_id(0)

    @pl.when(k == 0)
    def _():
        acc[...] = jnp.zeros_like(acc)

    for j in range(2):
        x = x_ref[:, j].reshape(1024, 1024)
        at = pl.ds(1024 * j, 1024)
        e = jnp.concatenate([e_ref[0, at], e_ref[1, at]], axis=1)
        acc[...] += jnp.dot(x, e, preferred_element_type=F32)

    @pl.when(k == pl.num_programs(0) - 1)
    def _():
        for j in range(2):
            o_ref[j] = jnp.dot(
                s_ref[j], acc[:, 128 * j : 128 * (j + 1)].astype(BF), preferred_element_type=F32
            ).astype(BF)


def low_own_rows(every, entry, select):
    return pl.pallas_call(
        low_kernel,
        grid=(4,),
        in_specs=[
            pl.BlockSpec((16, 2, 64, 1024), lambda k: (0, k, 0, 0)),
            pl.BlockSpec((2, 2048, 128), lambda k: (0, k, 0)),
            pl.BlockSpec((2, SEGMENT, 1024), lambda k: (0, 0, 0)),
        ],
        out_specs=pl.BlockSpec((2, SEGMENT, 128), lambda k: (0, 0, 0)),
        out_shape=jax.ShapeDtypeStruct((2, SEGMENT, 128), BF),
        scratch_shapes=[pltpu.VMEM((1024, 256), F32)],
        compiler_params=params(),
        cost_estimate=pl.CostEstimate(
            flops=2 * 1024 * 8192 * 256, bytes_accessed=21 << 20, transcendentals=0
        ),
        name="low_own",
    )(every, entry, select)


def gate_up_kernel(x_ref, g_ref, u_ref, go_ref, uo_ref):
    k = pl.program_id(0)

    @pl.when(k == 0)
    def _():
        go_ref[...] = jnp.zeros_like(go_ref)
        uo_ref[...] = jnp.zeros_like(uo_ref)

    for j in range(2):
        x = x_ref[:, j].reshape(1024, 1024)
        at = pl.ds(1024 * j, 1024)
        go_ref[...] += nt(x, g_ref[:, at])
        uo_ref[...] += nt(x, u_ref[:, at])


def gate_up(every, gate, up):
    n = gate.shape[0]
    return pl.pallas_call(
        gate_up_kernel,
        grid=(4,),
        in_specs=[
            pl.BlockSpec((16, 2, 64, 1024), lambda k: (0, k, 0, 0)),
            pl.BlockSpec((n, 2048), lambda k: (0, k)),
            pl.BlockSpec((n, 2048), lambda k: (0, k)),
        ],
        out_specs=[pl.BlockSpec((1024, n), lambda k: (0, 0))] * 2,
        out_shape=[jax.ShapeDtypeStruct((1024, n), F32)] * 2,
        compiler_params=params(),
        cost_estimate=pl.CostEstimate(
            flops=2 * 1024 * 8192 * 512, bytes_accessed=25 << 20, transcendentals=0
        ),
        name="gate_up",
    )(every, gate, up)


def hidden_kernel(
    place, g_ref, u_ref, q_ref, m_ref, low_ref, ge_ref, ue_ref, de_ref, h_ref, t_ref
):
    low = jnp.dot(q_ref[...], low_ref[...], preferred_element_type=F32)
    lg = low[:, :64].astype(BF)
    lu = low[:, 64:].astype(BF)
    lg = jnp.concatenate([lg] * 4, axis=1)
    lu = jnp.concatenate([lu] * 4, axis=1)
    gate = g_ref[...]
    up = u_ref[...]
    for j in range(8):
        mask = m_ref[:, 256 * j : 256 * (j + 1)]
        gate += jnp.dot(lg * mask, ge_ref[pl.ds(256 * j, 256)], preferred_element_type=F32)
        up += jnp.dot(lu * mask, ue_ref[pl.ds(256 * j, 256)], preferred_element_type=F32)
    hidden = (gate / (1.0 + jnp.exp(-gate)) * up).astype(BF)
    down = jnp.zeros((256, 256), F32)
    for j in range(8):
        mask = m_ref[:, 256 * j : 256 * (j + 1)].astype(F32)
        down += nt(hidden, de_ref[pl.ds(256 * j, 256)]) * mask
    down = (down[:, :128] + down[:, 128:]).astype(BF)
    wide = jnp.concatenate([hidden, jnp.zeros((256, 256 - hidden.shape[1]), BF), down], axis=1)
    ry = place[pl.program_id(0)]
    for z in range(4):
        rz = place[4 + z]
        upper = wide[64 * z : 64 * z + 32]
        lower = wide[64 * z + 32 : 64 * z + 64]
        h_ref[(rz + 3) % 4, 0, ry] = upper
        h_ref[(ry + 3) % 4, 1, rz] = lower
        t_ref[(7 - rz) % 4, 0, (4 - ry) % 4] = upper
        t_ref[(7 - ry) % 4, 1, (4 - rz) % 4] = lower


def hidden_rows(place, gate, up, pick, mask, low, gate_exit, up_exit, down_entry):
    n = gate.shape[1]
    return pl.pallas_call(
        hidden_kernel,
        grid_spec=pltpu.PrefetchScalarGridSpec(
            num_scalar_prefetch=1,
            grid=(4,),
            in_specs=[
                pl.BlockSpec((256, n), lambda i, p: (i, 0)),
                pl.BlockSpec((256, n), lambda i, p: (i, 0)),
                pl.BlockSpec((256, 2560), lambda i, p: (i, 0)),
                pl.BlockSpec((256, 2048), lambda i, p: (i, 0)),
                pl.BlockSpec((2560, 128), lambda i, p: (0, 0)),
                pl.BlockSpec((2048, n), lambda i, p: (0, 0)),
                pl.BlockSpec((2048, n), lambda i, p: (0, 0)),
                pl.BlockSpec((2048, n), lambda i, p: (0, 0)),
            ],
            out_specs=[pl.BlockSpec((4, 2, 4, 32, 384), lambda i, p: (0, 0, 0, 0, 0))] * 2,
        ),
        out_shape=[jax.ShapeDtypeStruct((4, 2, 4, 32, 384), BF)] * 2,
        compiler_params=params(),
        cost_estimate=pl.CostEstimate(
            flops=2 * 1024 * 2560 * 512, bytes_accessed=16 << 20, transcendentals=1024 * n
        ),
        name="hidden_rows",
    )(place, gate, up, pick, mask, low, gate_exit, up_exit, down_entry)


def on_device(
    tokens,
    token_adapter,
    adapter_slot_table,
    gate_matrix,
    up_matrix,
    down_matrix,
    adapter_entry_maps,
    adapter_gate_exit,
    adapter_up_exit,
    adapter_down_entry,
    adapter_down_exit,
):
    units = gate_matrix.shape[1]
    a = lax.axis_index("adapter")
    t = lax.axis_index("tensor")
    y, z, x, c = a // 4, a % 4, t // 2, t % 2
    way = 1 - 2 * c

    every = lax.all_gather(tokens, AXES, axis=0, tiled=False).reshape(16, 8, 64, 1024)
    ids = lax.all_gather(token_adapter, "adapter", axis=0, tiled=True)

    exits = []
    for kept, axes in ((0, "yz"), (1, "zy")):
        held = adapter_down_exit[kept]
        for axis in axes:
            held = [held]
            for _ in range(3):
                held.append(ring(held[-1], axis))
            held = jnp.stack(held)
        exits.append(held.reshape(1024, 1024))
    every, exits = lax.optimization_barrier((every, exits))

    names = jnp.arange(32, dtype=jnp.int32)
    member = ids[:, None] == names[None, :]
    order = jnp.arange(1024, dtype=jnp.int32)
    before = (order[:, None] > order[None, :]).astype(BF)
    earlier = jnp.dot(before, member.astype(BF), preferred_element_type=F32).astype(jnp.int32)
    rank_in = jnp.sum(jnp.where(member, earlier, 0), axis=1)
    slot = jnp.sum(jnp.where(member, adapter_slot_table[None, :], 0), axis=1)
    owner = slot // 2
    row = (slot % 2) * SEGMENT + rank_in
    select = (
        (jnp.where(owner == a, row, -1))[None, :] == jnp.arange(160, dtype=jnp.int32)[:, None]
    ).astype(BF).reshape(2, SEGMENT, 1024)
    relative = ((owner % 4 - z) % 4) * 4 + (owner // 4 - y) % 4
    pick = (
        (relative * 160 + row)[:, None] == jnp.arange(2560, dtype=jnp.int32)[None, :]
    ).astype(BF)
    mask = (slot[:, None] == (jnp.arange(2048, dtype=jnp.int32) // 64)[None, :]).astype(BF)

    def column(r, core):
        at = ((x + r) % 4 * 2 + core) * 1024
        return lax.dynamic_slice(down_matrix, (0, at), (units, 1024))

    turns = (1, 2, 3, 0)
    extra = jnp.pad(jnp.eye(128, dtype=BF), ((256, 0), (0, 0)))

    def columns(turns, core):
        return jnp.pad(
            jnp.concatenate([column(r, core) for r in turns], axis=1), ((0, 384 - units), (0, 0))
        )

    theirs = jnp.concatenate([columns(turns, 1 - c), extra], axis=1)
    mine = (columns((1, 2), c)[:256], jnp.concatenate([columns((3, 0), c), extra], axis=1))

    low_own = low_own_rows(every, adapter_entry_maps, select).reshape(160, 128)
    low = jnp.stack([low_own] + [send(low_own, dy=-d) for d in (1, 2, 3)])
    low = jnp.stack([low] + [send(low, dz=-d) for d in (1, 2, 3)]).reshape(2560, 128)
    gate, up = gate_up(every, gate_matrix.T, up_matrix.T)

    quarter = jnp.arange(4, dtype=jnp.int32)
    place = jnp.concatenate([way * (y - quarter) % 4, way * (z - quarter) % 4])
    rows, back = hidden_rows(
        place,
        gate,
        up,
        pick,
        mask,
        low,
        adapter_gate_exit.reshape(2048, units),
        adapter_up_exit.reshape(2048, units),
        adapter_down_entry.transpose(0, 2, 1).reshape(2048, units),
    )
    rows = rows.reshape(4, 2, 128, 384)
    back = back.reshape(4, 256, 384)
    first = jnp.dot(back[0], theirs, preferred_element_type=F32).astype(BF)
    back, first = lax.optimization_barrier((back, first))
    rest = jnp.dot(back[1:].reshape(768, 384), theirs, preferred_element_type=F32).astype(BF)
    rest, first_other = lax.optimization_barrier((rest, send(first, dc=1)))
    others = jnp.split(send(rest, dc=1).reshape(3, 2, 128, 4224), 3)
    others = [first_other.reshape(1, 2, 128, 4224)] + others

    axes = (("z", "y"), ("y", "z"))
    spans = ((0, 2048), (2048, 4224))

    def own_part(step, ch, color, lo=0, hi=128):
        h = rows[step, color, lo:hi, : mine[ch].shape[0]]
        part = jnp.dot(h, mine[ch], preferred_element_type=F32)
        return part + others[step][0, color, lo:hi, slice(*spans[ch])].astype(F32)

    chains = [(ch, color) for ch in range(2) for color in range(2)]
    came = {}
    for step in range(3):
        for ch, color in chains:
            total = own_part(step, ch, color)
            if step > 0:
                total += came[ch, color].astype(F32)
            came[ch, color] = ring(total.astype(BF), axes[color][0])
    state = {}
    for r in turns:
        for ch, color in chains:
            total = own_part(3, ch, color, 32 * r, 32 * r + 32)
            total += came[ch, color][32 * r : 32 * r + 32].astype(F32)
            if r != 1:
                total += state[ch, color].astype(F32)
            state[ch, color] = ring(total.astype(BF), axes[color][1]) if r != 0 else total
    summed = [jnp.concatenate([state[ch, 0], state[ch, 1]]) for ch in range(2)]
    tail = summed[1][:, 2048:]
    blocks = {
        1: summed[0][:, :1024],
        2: summed[0][:, 1024:],
        3: summed[1][:, :1024],
        0: summed[1][:, 1024:2048],
    }
    total = jnp.concatenate([blocks[0], tail], axis=1)
    for r in (1, 2, 3):
        total = total + send(
            jnp.concatenate([blocks[r], tail], axis=1).astype(BF), dx=r
        ).astype(F32)

    own_slot = jnp.sum(
        jnp.where(token_adapter[:, None] == names[None, :], adapter_slot_table[None, :], 0), axis=1
    )
    low_down = total[:, 1024:].astype(BF)
    ry = way * (y - own_slot // 8) % 4
    rz = way * (z - own_slot // 2 % 4) % 4
    at = jnp.arange(1024, dtype=jnp.int32) // 64
    result = total[:, :1024]
    for kept, relative in enumerate((rz * 4 + ry, ry * 4 + rz)):
        spread = jnp.tile(low_down[:, 64 * kept : 64 * kept + 64], (1, 16))
        spread = jnp.where(relative[:, None] == at[None, :], spread, 0)
        result += jnp.dot(spread, exits[kept], preferred_element_type=F32)
    return result.astype(BF)


def solution(mesh):
    return jax.shard_map(
        on_device,
        mesh=mesh,
        in_specs=(
            P("adapter", "tensor"),
            P("adapter"),
            P(),
            P(None, ("adapter", "tensor")),
            P(None, ("adapter", "tensor")),
            P(("adapter", "tensor"), None),
            P("adapter", None, None),
            P(None, None, ("adapter", "tensor")),
            P(None, None, ("adapter", "tensor")),
            P(None, ("adapter", "tensor"), None),
            P("adapter", None, "tensor"),
        ),
        out_specs=P("adapter", "tensor"),
        check_vma=False,
    )
```

```python
import functools

import jax
import jax.numpy as jnp
from jax import lax
from jax.experimental import pallas as pl
from jax.experimental.pallas import tpu as pltpu
from jax.sharding import PartitionSpec as P

SEGMENT = 80
BF = jnp.bfloat16
F32 = jnp.float32
AXES = ("adapter", "tensor")
VMEM_LIMIT = 60 * 1024 * 1024


def pairs(move):
    out = []
    for i in range(128):
        y, z, x, c = i // 32, (i // 8) % 4, (i // 2) % 4, i % 2
        ty, tz, tx, tc = move(y, z, x, c)
        out.append((i, (ty % 4) * 32 + (tz % 4) * 8 + (tx % 4) * 2 + tc % 2))
    return out


def send(value, dy=0, dz=0, dx=0, dc=0):
    return lax.ppermute(value, AXES, pairs(lambda y, z, x, c: (y + dy, z + dz, x + dx, c + dc)))


def onward(value, axis, step):
    def move(y, z, x, c):
        d = step * (1 - 2 * c)
        return (y + d, z, x, c) if axis == "y" else (y, z + d, x, c)

    return lax.ppermute(value, AXES, pairs(move))


def ring(value, axis):
    return onward(value, axis, 1)


def params(n=1):
    return pltpu.CompilerParams(
        dimension_semantics=("arbitrary",) * n, vmem_limit_bytes=VMEM_LIMIT
    )


def nt(a, b):
    return lax.dot_general(a, b, (((1,), (1,)), ((), ())), preferred_element_type=F32)


def block_rows(ref, j, turn):
    if turn:
        return jnp.concatenate([ref[g, j] for g in (0, 3, 2, 1)], axis=0)
    return ref[:, j].reshape(128, 1024)


def arrival_kernel(turn, add, order, xa, xb, g0, g1, u0, u1, e0, e1, *refs):
    o_ref = refs[-1]

    @pl.when(pl.program_id(0) == 0)
    def _():
        o_ref[...] = refs[0][...] if add else jnp.zeros_like(o_ref)

    n = g0.shape[0]
    for j, (g, u, e) in enumerate(((g0, u0, e0), (g1, u1, e1))):
        x = jnp.concatenate([block_rows(xa, j, turn), block_rows(xb, j, turn)], axis=0)
        o_ref[0, :, :n] += nt(x, g[...])
        o_ref[0, :, 256 : 256 + n] += nt(x, u[...])
        entry = jnp.concatenate([e[0], e[1]], axis=1)
        o_ref[0, :, 512:] += jnp.dot(x, entry, preferred_element_type=F32)


def arrival(order, xa, xb, gate, up, entry, sums, block, turn, add):
    n = gate.shape[0]
    specs = [pl.BlockSpec((4, 2, 32, 1024), lambda i, p: (0, i, 0, 0))] * 2
    for _ in range(2):
        for j in range(2):
            specs.append(pl.BlockSpec((n, 1024), lambda i, p, j=j: (0, p[2 * i + j])))
    for j in range(2):
        specs.append(pl.BlockSpec((2, 1024, 128), lambda i, p, j=j: (0, p[2 * i + j], 0)))
    place = pl.BlockSpec((1, 256, 768), lambda i, p: (block, 0, 0))
    args = [order, xa, xb, gate, gate, up, up, entry, entry]
    alias = {}
    if sums is not None:
        specs.append(place if add else pl.BlockSpec(memory_space=pl.ANY))
        alias = {len(args): 0}
        args.append(sums)
    return pl.pallas_call(
        functools.partial(arrival_kernel, turn, add),
        grid_spec=pltpu.PrefetchScalarGridSpec(
            num_scalar_prefetch=1, grid=(2,), in_specs=specs, out_specs=place
        ),
        out_shape=jax.ShapeDtypeStruct((4, 256, 768), F32),
        input_output_aliases=alias,
        compiler_params=params(),
        cost_estimate=pl.CostEstimate(
            flops=2 * 256 * 4096 * 768, bytes_accessed=9 << 20, transcendentals=0
        ),
        name="arrival",
    )(*args)


def low_kernel(l_ref, s_ref, o_ref):
    for j in range(2):
        total = jnp.zeros((SEGMENT, 128), F32)
        for r in range(4):
            total += jnp.dot(
                s_ref[j, :, 256 * r : 256 * (r + 1)],
                l_ref[r, :, 128 * j : 128 * (j + 1)].astype(BF),
                preferred_element_type=F32,
            )
        o_ref[j] = total.astype(BF)


def low_own_rows(sums, select):
    return pl.pallas_call(
        low_kernel,
        grid=(1,),
        in_specs=[
            pl.BlockSpec((4, 256, 256), lambda k: (0, 0, 2)),
            pl.BlockSpec((2, SEGMENT, 1024), lambda k: (0, 0, 0)),
        ],
        out_specs=pl.BlockSpec((2, SEGMENT, 128), lambda k: (0, 0, 0)),
        out_shape=jax.ShapeDtypeStruct((2, SEGMENT, 128), BF),
        compiler_params=params(),
        cost_estimate=pl.CostEstimate(
            flops=2 * 1024 * 160 * 128, bytes_accessed=2 << 20, transcendentals=0
        ),
        name="low_own",
    )(sums, select)


def hidden_kernel(a_ref, q_ref, m_ref, low_ref, ge_ref, ue_ref, de_ref, h_ref, t_ref):
    n = ge_ref.shape[1]
    low = jnp.dot(q_ref[...], low_ref[...], preferred_element_type=F32)
    lg = low[:, :64].astype(BF)
    lu = low[:, 64:].astype(BF)
    lg = jnp.concatenate([lg] * 4, axis=1)
    lu = jnp.concatenate([lu] * 4, axis=1)
    gate = a_ref[0, :, :n]
    up = a_ref[0, :, 256 : 256 + n]
    for j in range(8):
        mask = m_ref[:, 256 * j : 256 * (j + 1)]
        gate += jnp.dot(lg * mask, ge_ref[pl.ds(256 * j, 256)], preferred_element_type=F32)
        up += jnp.dot(lu * mask, ue_ref[pl.ds(256 * j, 256)], preferred_element_type=F32)
    hidden = (gate / (1.0 + jnp.exp(-gate)) * up).astype(BF)
    down = jnp.zeros((256, 256), F32)
    for j in range(8):
        mask = m_ref[:, 256 * j : 256 * (j + 1)].astype(F32)
        down += nt(hidden, de_ref[pl.ds(256 * j, 256)]) * mask
    down = (down[:, :128] + down[:, 128:]).astype(BF)
    wide = jnp.concatenate([hidden, jnp.zeros((256, 256 - n), BF), down], axis=1)
    for color in range(2):
        for group in range(4):
            at = 128 * color + 32 * group
            h_ref[0, color, group] = wide[at : at + 32]
            t_ref[0, color, (4 - group) % 4] = wide[at : at + 32]


def hidden_rows(sums, pick, mask, low, gate_exit, up_exit, down_entry):
    n = gate_exit.shape[1]
    return pl.pallas_call(
        hidden_kernel,
        grid=(4,),
        in_specs=[
            pl.BlockSpec((1, 256, 512), lambda i: (i, 0, 0)),
            pl.BlockSpec((256, 2560), lambda i: (i, 0)),
            pl.BlockSpec((256, 2048), lambda i: (i, 0)),
            pl.BlockSpec((2560, 128), lambda i: (0, 0)),
            pl.BlockSpec((2048, n), lambda i: (0, 0)),
            pl.BlockSpec((2048, n), lambda i: (0, 0)),
            pl.BlockSpec((2048, n), lambda i: (0, 0)),
        ],
        out_specs=[
            pl.BlockSpec((1, 2, 4, 32, 384), lambda i: ((i + 3) % 4, 0, 0, 0, 0)),
            pl.BlockSpec((1, 2, 4, 32, 384), lambda i: ((7 - i) % 4, 0, 0, 0, 0)),
        ],
        out_shape=[jax.ShapeDtypeStruct((4, 2, 4, 32, 384), BF)] * 2,
        compiler_params=params(),
        cost_estimate=pl.CostEstimate(
            flops=2 * 1024 * 2560 * 512, bytes_accessed=16 << 20, transcendentals=1024 * n
        ),
        name="hidden_rows",
    )(sums, pick, mask, low, gate_exit, up_exit, down_entry)


def on_device(
    tokens,
    token_adapter,
    adapter_slot_table,
    gate_matrix,
    up_matrix,
    down_matrix,
    adapter_entry_maps,
    adapter_gate_exit,
    adapter_up_exit,
    adapter_down_entry,
    adapter_down_exit,
):
    units = gate_matrix.shape[1]
    a = lax.axis_index("adapter")
    t = lax.axis_index("tensor")
    y, z, x, c = a // 4, a % 4, t // 2, t % 2
    way = 1 - 2 * c

    near = jnp.stack([tokens] + [send(tokens, dx=-d) for d in (1, 2, 3)])
    known = token_adapter
    for axis in "yz":
        known = jnp.stack([known] + [onward(known, axis, d) for d in (1, 2, 3)])
    exits = lax.all_gather(adapter_down_exit, "adapter", axis=0, tiled=True).reshape(2048, 1024)

    quarter = jnp.arange(4, dtype=jnp.int32)

    def column(r, core):
        at = ((x + r) % 4 * 2 + core) * 1024
        return lax.dynamic_slice(down_matrix, (0, at), (units, 1024))

    turns = (1, 2, 3, 0)

    def columns(turns, core, rows, extra):
        width = 1024 * len(turns)
        if extra:
            out = jnp.pad(jnp.eye(128, dtype=BF), ((rows - 128, 0), (width, 0)))
        else:
            out = jnp.zeros((rows, width), BF)
        for i, r in enumerate(turns):
            out = lax.dynamic_update_slice(out, column(r, core), (0, 1024 * i))
        return out

    theirs = columns(turns, 1 - c, 384, True)
    mine = (columns((1, 2), c, 256, False), columns((3, 0), c, 384, True))

    gate_t, up_t = gate_matrix.T, up_matrix.T
    group = (x + quarter) % 4 * 2
    halves = [near[:, :32], near[:, 32:]]
    blocks = [halves]
    for _ in range(3):
        blocks.append([ring(v, axis) for v, axis in zip(blocks[-1], "yz")])
    held = [jnp.stack([b[k] for b in blocks]) for k in range(2)]
    held, known = lax.optimization_barrier((held, known))
    across, down = (y - way * quarter) % 4, (z - way * quarter) % 4
    homes = across[None, :] * 4 + down[:, None]
    order = homes[:, :, None] * 64 + jnp.arange(64, dtype=jnp.int32)

    def blockwise(v):
        return jnp.stack([v[:, :, :32], v[:, :, 32:].swapaxes(0, 1)], axis=1).reshape(1024)

    ids, order = blockwise(known), blockwise(order)
    names = jnp.arange(32, dtype=jnp.int32)
    member = ids[:, None] == names[None, :]
    before = (order[:, None] > order[None, :]).astype(BF)
    earlier = jnp.dot(before, member.astype(BF), preferred_element_type=F32).astype(jnp.int32)
    rank_in = jnp.sum(jnp.where(member, earlier, 0), axis=1)
    slot = jnp.sum(jnp.where(member, adapter_slot_table[None, :], 0), axis=1)
    row = (slot % 2) * SEGMENT + rank_in
    owner = slot // 2
    select = (
        (jnp.where(owner == a, row, -1))[None, :] == jnp.arange(160, dtype=jnp.int32)[:, None]
    ).astype(BF).reshape(2, SEGMENT, 1024)
    relative = ((owner % 4 - z) % 4) * 4 + (owner // 4 - y) % 4
    pick = (
        (relative * 160 + row)[:, None] == jnp.arange(2560, dtype=jnp.int32)[None, :]
    ).astype(BF)
    mask = (slot[:, None] == (jnp.arange(2048, dtype=jnp.int32) // 64)[None, :]).astype(BF)

    sums = None
    for r in range(4):
        following = [ring(v, axis) for v, axis in zip(held, "zy")] if r < 3 else None
        sums = arrival(
            group + c, *held, gate_t, up_t, adapter_entry_maps, sums, r, False, r == 3
        )
        other = [send(v, dc=1) for v in held]
        sums = arrival(
            group + 1 - c, *other, gate_t, up_t, adapter_entry_maps, sums, (4 - r) % 4, True, r != 1
        )
        if r < 3:
            held, sums = lax.optimization_barrier((following, sums))

    low_own = low_own_rows(sums, select).reshape(160, 128)
    low = jnp.stack([low_own] + [send(low_own, dy=-d) for d in (1, 2, 3)])
    low = jnp.stack([low] + [send(low, dz=-d) for d in (1, 2, 3)]).reshape(2560, 128)
    low, exits = lax.optimization_barrier((low, exits))
    rows, back = hidden_rows(
        sums,
        pick,
        mask,
        low,
        adapter_gate_exit.reshape(2048, units),
        adapter_up_exit.reshape(2048, units),
        adapter_down_entry.transpose(0, 2, 1).reshape(2048, units),
    )
    rows = rows.reshape(4, 2, 128, 384)
    back = back.reshape(4, 256, 384)
    first = jnp.dot(back[0], theirs, preferred_element_type=F32).astype(BF)
    back, first = lax.optimization_barrier((back, first))
    rest = jnp.dot(back[1:].reshape(768, 384), theirs, preferred_element_type=F32).astype(BF)
    rest, first_other = lax.optimization_barrier((rest, send(first, dc=1)))
    others = jnp.split(send(rest, dc=1).reshape(3, 2, 128, 4224), 3)
    others = [first_other.reshape(1, 2, 128, 4224)] + others

    axes = (("z", "y"), ("y", "z"))
    spans = ((0, 2048), (2048, 4224))

    def own_part(step, ch, color, lo=0, hi=128):
        h = rows[step, color, lo:hi, : mine[ch].shape[0]]
        part = jnp.dot(h, mine[ch], preferred_element_type=F32)
        return part + others[step][0, color, lo:hi, slice(*spans[ch])].astype(F32)

    chains = [(ch, color) for ch in range(2) for color in range(2)]
    came = {}
    for step in range(3):
        for ch, color in chains:
            total = own_part(step, ch, color)
            if step > 0:
                total += came[ch, color].astype(F32)
            came[ch, color] = ring(total.astype(BF), axes[color][0])
    state = {}
    for r in turns:
        for ch, color in chains:
            total = own_part(3, ch, color, 32 * r, 32 * r + 32)
            total += came[ch, color][32 * r : 32 * r + 32].astype(F32)
            if r != 1:
                total += state[ch, color].astype(F32)
            state[ch, color] = ring(total.astype(BF), axes[color][1]) if r != 0 else total
    summed = [jnp.concatenate([state[ch, 0], state[ch, 1]]) for ch in range(2)]
    tail = summed[1][:, 2048:]
    blocks = {
        1: summed[0][:, :1024],
        2: summed[0][:, 1024:],
        3: summed[1][:, :1024],
        0: summed[1][:, 1024:2048],
    }
    total = jnp.concatenate([blocks[0], tail], axis=1)
    for r in (1, 2, 3):
        total = total + send(
            jnp.concatenate([blocks[r], tail], axis=1).astype(BF), dx=r
        ).astype(F32)

    own_slot = jnp.sum(
        jnp.where(token_adapter[:, None] == names[None, :], adapter_slot_table[None, :], 0), axis=1
    )
    low_down = total[:, 1024:].astype(BF)
    spread = jnp.tile(low_down, (1, 16))
    at = jnp.arange(2048, dtype=jnp.int32) // 128
    spread = jnp.where((own_slot // 2)[:, None] == at[None, :], spread, 0)
    delta = jnp.dot(spread, exits, preferred_element_type=F32)
    return (total[:, :1024] + delta).astype(BF)


def solution(mesh):
    return jax.shard_map(
        on_device,
        mesh=mesh,
        in_specs=(
            P("adapter", "tensor"),
            P("adapter"),
            P(),
            P(None, ("adapter", "tensor")),
            P(None, ("adapter", "tensor")),
            P(("adapter", "tensor"), None),
            P("adapter", None, None),
            P(None, None, ("adapter", "tensor")),
            P(None, None, ("adapter", "tensor")),
            P(None, ("adapter", "tensor"), None),
            P("adapter", None, "tensor"),
        ),
        out_specs=P("adapter", "tensor"),
        check_vma=False,
    )
```

```python
import functools

import jax
import jax.numpy as jnp
from jax import lax
from jax.experimental import pallas as pl
from jax.experimental.pallas import tpu as pltpu
from jax.sharding import PartitionSpec as P

SEGMENT = 80
BF = jnp.bfloat16
F32 = jnp.float32
AXES = ("adapter", "tensor")
VMEM_LIMIT = 60 * 1024 * 1024


def pairs(move):
    out = []
    for i in range(128):
        y, z, x, c = i // 32, (i // 8) % 4, (i // 2) % 4, i % 2
        ty, tz, tx, tc = move(y, z, x, c)
        out.append((i, (ty % 4) * 32 + (tz % 4) * 8 + (tx % 4) * 2 + tc % 2))
    return out


def send(value, dy=0, dz=0, dx=0, dc=0):
    return lax.ppermute(value, AXES, pairs(lambda y, z, x, c: (y + dy, z + dz, x + dx, c + dc)))


def onward(value, axis, step):
    def move(y, z, x, c):
        d = step * (1 - 2 * c)
        return (y + d, z, x, c) if axis == "y" else (y, z + d, x, c)

    return lax.ppermute(value, AXES, pairs(move))


def ring(value, axis):
    return onward(value, axis, 1)


def params(n=1):
    return pltpu.CompilerParams(
        dimension_semantics=("arbitrary",) * n, vmem_limit_bytes=VMEM_LIMIT
    )


def nt(a, b):
    return lax.dot_general(a, b, (((1,), (1,)), ((), ())), preferred_element_type=F32)


def block_rows(ref, j, turn):
    if turn:
        return jnp.concatenate([ref[g, j] for g in (0, 3, 2, 1)], axis=0)
    return ref[:, j].reshape(128, 1024)


def arrival_kernel(turn, add, low, order, xa, xb, *refs):
    o_ref = refs[-1]

    @pl.when(pl.program_id(0) == 0)
    def _():
        o_ref[...] = refs[-2][...] if add else jnp.zeros_like(o_ref)

    for j in range(2):
        x = jnp.concatenate([block_rows(xa, j, turn), block_rows(xb, j, turn)], axis=0)
        if low:
            e = refs[j]
            entry = jnp.concatenate([e[0], e[1]], axis=1)
            o_ref[0] += jnp.dot(x, entry, preferred_element_type=F32)
        else:
            g, u = refs[j], refs[2 + j]
            n = g.shape[0]
            o_ref[0, :, :n] += nt(x, g[...])
            o_ref[0, :, 256 : 256 + n] += nt(x, u[...])


def arrival(order, held, weights, sums, block, turn, add):
    low = len(weights) == 1
    specs = [pl.BlockSpec((4, 2, 32, 1024), lambda i, p: (0, i, 0, 0))] * 2
    args = [order, *held]
    for w in weights:
        for j in range(2):
            if low:
                specs.append(pl.BlockSpec((2, 1024, 128), lambda i, p, j=j: (0, p[2 * i + j], 0)))
            else:
                specs.append(
                    pl.BlockSpec((w.shape[0], 1024), lambda i, p, j=j: (0, p[2 * i + j]))
                )
            args.append(w)
    width = 256 * len(weights)
    place = pl.BlockSpec((1, 256, width), lambda i, p: (block, 0, 0))
    alias = {}
    if sums is not None:
        specs.append(place if add else pl.BlockSpec(memory_space=pl.ANY))
        alias = {len(args): 0}
        args.append(sums)
    return pl.pallas_call(
        functools.partial(arrival_kernel, turn, add, low),
        grid_spec=pltpu.PrefetchScalarGridSpec(
            num_scalar_prefetch=1, grid=(2,), in_specs=specs, out_specs=place
        ),
        out_shape=jax.ShapeDtypeStruct((4, 256, width), F32),
        input_output_aliases=alias,
        compiler_params=params(),
        cost_estimate=pl.CostEstimate(
            flops=2 * 256 * 4096 * width,
            bytes_accessed=(4 << 20) + 8192 * width,
            transcendentals=0,
        ),
        name="low_arrival" if low else "arrival",
    )(*args)


def low_kernel(l_ref, s_ref, o_ref):
    for j in range(2):
        total = jnp.zeros((SEGMENT, 128), F32)
        for r in range(4):
            total += jnp.dot(
                s_ref[j, :, 256 * r : 256 * (r + 1)],
                l_ref[r, :, 128 * j : 128 * (j + 1)].astype(BF),
                preferred_element_type=F32,
            )
        o_ref[j] = total.astype(BF)


def low_own_rows(sums, select):
    return pl.pallas_call(
        low_kernel,
        grid=(1,),
        in_specs=[
            pl.BlockSpec((4, 256, 256), lambda k: (0, 0, 0)),
            pl.BlockSpec((2, SEGMENT, 1024), lambda k: (0, 0, 0)),
        ],
        out_specs=pl.BlockSpec((2, SEGMENT, 128), lambda k: (0, 0, 0)),
        out_shape=jax.ShapeDtypeStruct((2, SEGMENT, 128), BF),
        compiler_params=params(),
        cost_estimate=pl.CostEstimate(
            flops=2 * 1024 * 160 * 128, bytes_accessed=2 << 20, transcendentals=0
        ),
        name="low_own",
    )(sums, select)


def hidden_kernel(a_ref, q_ref, m_ref, low_ref, ge_ref, ue_ref, de_ref, h_ref, t_ref):
    n = ge_ref.shape[1]
    low = jnp.dot(q_ref[...], low_ref[...], preferred_element_type=F32)
    lg = low[:, :64].astype(BF)
    lu = low[:, 64:].astype(BF)
    lg = jnp.concatenate([lg] * 4, axis=1)
    lu = jnp.concatenate([lu] * 4, axis=1)
    gate = a_ref[0, :, :n]
    up = a_ref[0, :, 256 : 256 + n]
    for j in range(8):
        mask = m_ref[:, 256 * j : 256 * (j + 1)]
        gate += jnp.dot(lg * mask, ge_ref[pl.ds(256 * j, 256)], preferred_element_type=F32)
        up += jnp.dot(lu * mask, ue_ref[pl.ds(256 * j, 256)], preferred_element_type=F32)
    hidden = (gate / (1.0 + jnp.exp(-gate)) * up).astype(BF)
    down = jnp.zeros((256, 256), F32)
    for j in range(8):
        mask = m_ref[:, 256 * j : 256 * (j + 1)].astype(F32)
        down += nt(hidden, de_ref[pl.ds(256 * j, 256)]) * mask
    down = (down[:, :128] + down[:, 128:]).astype(BF)
    wide = jnp.concatenate([hidden, jnp.zeros((256, 256 - n), BF), down], axis=1)
    for color in range(2):
        for group in range(4):
            at = 128 * color + 32 * group
            h_ref[0, color, group] = wide[at : at + 32]
            t_ref[0, color, (4 - group) % 4] = wide[at : at + 32]


def hidden_rows(sums, pick, mask, low, gate_exit, up_exit, down_entry):
    n = gate_exit.shape[1]
    return pl.pallas_call(
        hidden_kernel,
        grid=(4,),
        in_specs=[
            pl.BlockSpec((1, 256, 512), lambda i: (i, 0, 0)),
            pl.BlockSpec((256, 2560), lambda i: (i, 0)),
            pl.BlockSpec((256, 2048), lambda i: (i, 0)),
            pl.BlockSpec((2560, 128), lambda i: (0, 0)),
            pl.BlockSpec((2048, n), lambda i: (0, 0)),
            pl.BlockSpec((2048, n), lambda i: (0, 0)),
            pl.BlockSpec((2048, n), lambda i: (0, 0)),
        ],
        out_specs=[
            pl.BlockSpec((1, 2, 4, 32, 384), lambda i: ((i + 3) % 4, 0, 0, 0, 0)),
            pl.BlockSpec((1, 2, 4, 32, 384), lambda i: ((7 - i) % 4, 0, 0, 0, 0)),
        ],
        out_shape=[jax.ShapeDtypeStruct((4, 2, 4, 32, 384), BF)] * 2,
        compiler_params=params(),
        cost_estimate=pl.CostEstimate(
            flops=2 * 1024 * 2560 * 512, bytes_accessed=16 << 20, transcendentals=1024 * n
        ),
        name="hidden_rows",
    )(sums, pick, mask, low, gate_exit, up_exit, down_entry)


def on_device(
    tokens,
    token_adapter,
    adapter_slot_table,
    gate_matrix,
    up_matrix,
    down_matrix,
    adapter_entry_maps,
    adapter_gate_exit,
    adapter_up_exit,
    adapter_down_entry,
    adapter_down_exit,
):
    units = gate_matrix.shape[1]
    a = lax.axis_index("adapter")
    t = lax.axis_index("tensor")
    y, z, x, c = a // 4, a % 4, t // 2, t % 2
    way = 1 - 2 * c

    near = jnp.stack([tokens] + [send(tokens, dx=-d) for d in (1, 2, 3)])
    kept = jnp.concatenate(
        [
            adapter_down_exit.reshape(128, 1024),
            jnp.pad(token_adapter.astype(BF)[None, :], ((0, 15), (0, 960))),
        ]
    )
    kept = lax.all_gather(kept, "adapter", axis=0, tiled=False)

    quarter = jnp.arange(4, dtype=jnp.int32)

    def column(r, core):
        at = ((x + r) % 4 * 2 + core) * 1024
        return lax.dynamic_slice(down_matrix, (0, at), (units, 1024))

    turns = (1, 2, 3, 0)

    def columns(turns, core, rows, extra):
        width = 1024 * len(turns)
        if extra:
            out = jnp.pad(jnp.eye(128, dtype=BF), ((rows - 128, 0), (width, 0)))
        else:
            out = jnp.zeros((rows, width), BF)
        for i, r in enumerate(turns):
            out = lax.dynamic_update_slice(out, column(r, core), (0, 1024 * i))
        return out

    theirs = columns(turns, 1 - c, 384, True)
    mine = (columns((1, 2), c, 256, False), columns((3, 0), c, 384, True))

    gate_t, up_t = gate_matrix.T, up_matrix.T
    group = (x + quarter) % 4 * 2
    halves = [near[:, :32], near[:, 32:]]
    blocks = [halves]
    for _ in range(3):
        blocks.append([ring(v, axis) for v, axis in zip(blocks[-1], "yz")])
    held = [jnp.stack([b[k] for b in blocks]) for k in range(2)]
    across, down = (y - way * quarter) % 4, (z - way * quarter) % 4
    homes = across[None, :] * 4 + down[:, None]
    order = homes[:, :, None] * 64 + jnp.arange(64, dtype=jnp.int32)

    known = kept[:, 128, :64].astype(jnp.int32)
    taken = homes.reshape(16, 1, 1) == jnp.arange(16, dtype=jnp.int32)[None, :, None]
    known = jnp.sum(jnp.where(taken, known[None], 0), axis=1).reshape(4, 4, 64)

    def blockwise(v):
        return jnp.stack([v[:, :, :32], v[:, :, 32:].swapaxes(0, 1)], axis=1).reshape(1024)

    ids, order = blockwise(known), blockwise(order)
    names = jnp.arange(32, dtype=jnp.int32)
    member = ids[:, None] == names[None, :]
    before = (order[:, None] > order[None, :]).astype(BF)
    earlier = jnp.dot(before, member.astype(BF), preferred_element_type=F32).astype(jnp.int32)
    rank_in = jnp.sum(jnp.where(member, earlier, 0), axis=1)
    slot = jnp.sum(jnp.where(member, adapter_slot_table[None, :], 0), axis=1)
    row = (slot % 2) * SEGMENT + rank_in
    owner = slot // 2
    select = (
        (jnp.where(owner == a, row, -1))[None, :] == jnp.arange(160, dtype=jnp.int32)[:, None]
    ).astype(BF).reshape(2, SEGMENT, 1024)
    relative = ((owner % 4 - z) % 4) * 4 + (owner // 4 - y) % 4
    pick = (
        (relative * 160 + row)[:, None] == jnp.arange(2560, dtype=jnp.int32)[None, :]
    ).astype(BF)
    mask = (slot[:, None] == (jnp.arange(2048, dtype=jnp.int32) // 64)[None, :]).astype(BF)

    mine_first = (group + c, False)
    theirs_next = (group + 1 - c, True)
    entry = (adapter_entry_maps,)
    gates = (gate_t, up_t)
    held, theirs, mine = lax.optimization_barrier((held, theirs, mine))
    low_sums, sums, late = None, None, []
    for r in range(4):
        following = [ring(v, axis) for v, axis in zip(held, "zy")] if r < 3 else None
        other = [send(v, dc=1) for v in held]
        for v, (features, turn), block, add in (
            (held, mine_first, r, r == 3),
            (other, theirs_next, (4 - r) % 4, r != 1),
        ):
            low_sums = arrival(features, v, entry, low_sums, block, turn, add)
            if r < 2:
                sums = arrival(features, v, gates, sums, block, turn, add)
            else:
                late.append((features, v, block, turn, add))
        if r < 2:
            held, low_sums, sums = lax.optimization_barrier((following, low_sums, sums))
        elif r < 3:
            held, low_sums, select, pick, mask = lax.optimization_barrier(
                (following, low_sums, select, pick, mask)
            )

    low_own = low_own_rows(low_sums, select)
    low_own, late = lax.optimization_barrier((low_own, [v for _, v, *_ in late])), late
    low_own, blocks = low_own
    for v, (features, _, block, turn, add) in zip(blocks, late):
        sums = arrival(features, v, gates, sums, block, turn, add)
    low_own = low_own.reshape(160, 128)
    low = jnp.stack([low_own] + [send(low_own, dy=-d) for d in (1, 2, 3)])
    low = jnp.stack([low] + [send(low, dz=-d) for d in (1, 2, 3)]).reshape(2560, 128)
    low, exits = lax.optimization_barrier((low, kept[:, :128].reshape(2048, 1024)))
    rows, back = hidden_rows(
        sums,
        pick,
        mask,
        low,
        adapter_gate_exit.reshape(2048, units),
        adapter_up_exit.reshape(2048, units),
        adapter_down_entry.transpose(0, 2, 1).reshape(2048, units),
    )
    rows = rows.reshape(4, 2, 128, 384)
    back = back.reshape(4, 256, 384)
    first = jnp.dot(back[0], theirs, preferred_element_type=F32).astype(BF)
    back, first = lax.optimization_barrier((back, first))
    rest = jnp.dot(back[1:].reshape(768, 384), theirs, preferred_element_type=F32).astype(BF)
    rest, first_other = lax.optimization_barrier((rest, send(first, dc=1)))
    others = jnp.split(send(rest, dc=1).reshape(3, 2, 128, 4224), 3)
    others = [first_other.reshape(1, 2, 128, 4224)] + others

    axes = (("z", "y"), ("y", "z"))
    spans = ((0, 2048), (2048, 4224))

    def own_part(step, ch, color, lo=0, hi=128):
        h = rows[step, color, lo:hi, : mine[ch].shape[0]]
        part = jnp.dot(h, mine[ch], preferred_element_type=F32)
        return part + others[step][0, color, lo:hi, slice(*spans[ch])].astype(F32)

    chains = [(ch, color) for ch in range(2) for color in range(2)]
    came = {}
    for step in range(3):
        for ch, color in chains:
            total = own_part(step, ch, color)
            if step > 0:
                total += came[ch, color].astype(F32)
            came[ch, color] = ring(total.astype(BF), axes[color][0])
    state = {}
    for r in turns:
        for ch, color in chains:
            total = own_part(3, ch, color, 32 * r, 32 * r + 32)
            total += came[ch, color][32 * r : 32 * r + 32].astype(F32)
            if r != 1:
                total += state[ch, color].astype(F32)
            state[ch, color] = ring(total.astype(BF), axes[color][1]) if r != 0 else total
    summed = [jnp.concatenate([state[ch, 0], state[ch, 1]]) for ch in range(2)]
    tail = summed[1][:, 2048:]
    blocks = {
        1: summed[0][:, :1024],
        2: summed[0][:, 1024:],
        3: summed[1][:, :1024],
        0: summed[1][:, 1024:2048],
    }
    total = jnp.concatenate([blocks[0], tail], axis=1)
    for r in (1, 2, 3):
        total = total + send(
            jnp.concatenate([blocks[r], tail], axis=1).astype(BF), dx=r
        ).astype(F32)

    own_slot = jnp.sum(
        jnp.where(token_adapter[:, None] == names[None, :], adapter_slot_table[None, :], 0), axis=1
    )
    low_down = total[:, 1024:].astype(BF)
    spread = jnp.tile(low_down, (1, 16))
    at = jnp.arange(2048, dtype=jnp.int32) // 128
    spread = jnp.where((own_slot // 2)[:, None] == at[None, :], spread, 0)
    delta = jnp.dot(spread, exits, preferred_element_type=F32)
    return (total[:, :1024] + delta).astype(BF)


def solution(mesh):
    return jax.shard_map(
        on_device,
        mesh=mesh,
        in_specs=(
            P("adapter", "tensor"),
            P("adapter"),
            P(),
            P(None, ("adapter", "tensor")),
            P(None, ("adapter", "tensor")),
            P(("adapter", "tensor"), None),
            P("adapter", None, None),
            P(None, None, ("adapter", "tensor")),
            P(None, None, ("adapter", "tensor")),
            P(None, ("adapter", "tensor"), None),
            P("adapter", None, "tensor"),
        ),
        out_specs=P("adapter", "tensor"),
        check_vma=False,
    )
```

```python
import functools

import jax
import jax.numpy as jnp
from jax import lax
from jax.experimental import pallas as pl
from jax.experimental.pallas import tpu as pltpu
from jax.sharding import PartitionSpec as P

SEGMENT = 80
BF = jnp.bfloat16
F32 = jnp.float32
AXES = ("adapter", "tensor")
VMEM_LIMIT = 60 * 1024 * 1024


def pairs(move):
    out = []
    for i in range(128):
        y, z, x, c = i // 32, (i // 8) % 4, (i // 2) % 4, i % 2
        ty, tz, tx, tc = move(y, z, x, c)
        out.append((i, (ty % 4) * 32 + (tz % 4) * 8 + (tx % 4) * 2 + tc % 2))
    return out


def send(value, dy=0, dz=0, dx=0, dc=0):
    return lax.ppermute(value, AXES, pairs(lambda y, z, x, c: (y + dy, z + dz, x + dx, c + dc)))


def onward(value, axis, step):
    def move(y, z, x, c):
        d = step * (1 - 2 * c)
        return (y + d, z, x, c) if axis == "y" else (y, z + d, x, c)

    return lax.ppermute(value, AXES, pairs(move))


def ring(value, axis):
    return onward(value, axis, 1)


def params(n=1):
    return pltpu.CompilerParams(
        dimension_semantics=("arbitrary",) * n, vmem_limit_bytes=VMEM_LIMIT
    )


def nt(a, b):
    return lax.dot_general(a, b, (((1,), (1,)), ((), ())), preferred_element_type=F32)


def low_kernel(x_ref, e_ref, s_ref, o_ref, acc):
    k = pl.program_id(0)

    @pl.when(k == 0)
    def _():
        acc[...] = jnp.zeros_like(acc)

    for j in range(2):
        x = x_ref[:, j].reshape(1024, 1024)
        at = pl.ds(1024 * j, 1024)
        e = jnp.concatenate([e_ref[0, at], e_ref[1, at]], axis=1)
        acc[...] += jnp.dot(x, e, preferred_element_type=F32)

    @pl.when(k == pl.num_programs(0) - 1)
    def _():
        for j in range(2):
            o_ref[j] = jnp.dot(
                s_ref[j], acc[:, 128 * j : 128 * (j + 1)].astype(BF), preferred_element_type=F32
            ).astype(BF)


def low_own_rows(every, entry, select):
    return pl.pallas_call(
        low_kernel,
        grid=(4,),
        in_specs=[
            pl.BlockSpec((16, 2, 64, 1024), lambda k: (0, k, 0, 0)),
            pl.BlockSpec((2, 2048, 128), lambda k: (0, k, 0)),
            pl.BlockSpec((2, SEGMENT, 1024), lambda k: (0, 0, 0)),
        ],
        out_specs=pl.BlockSpec((2, SEGMENT, 128), lambda k: (0, 0, 0)),
        out_shape=jax.ShapeDtypeStruct((2, SEGMENT, 128), BF),
        scratch_shapes=[pltpu.VMEM((1024, 256), F32)],
        compiler_params=params(),
        cost_estimate=pl.CostEstimate(
            flops=2 * 1024 * 8192 * 256, bytes_accessed=21 << 20, transcendentals=0
        ),
        name="low_own",
    )(every, entry, select)


def gate_up_kernel(x_ref, g_ref, u_ref, *refs):
    o_ref = refs[-1]
    n = g_ref.shape[0]

    @pl.when(pl.program_id(0) == 0)
    def _():
        o_ref[...] = jnp.zeros_like(o_ref)

    for j in range(2):
        x = x_ref[:, j].reshape(512, 1024)
        at = pl.ds(1024 * j, 1024)
        o_ref[0, :, :n] += nt(x, g_ref[:, at])
        o_ref[0, :, 256 : 256 + n] += nt(x, u_ref[:, at])


def gate_up(every, gate, up, half, sums):
    n = gate.shape[0]
    args = [every, gate, up]
    specs = [
        pl.BlockSpec((8, 2, 64, 1024), lambda k: (half, k, 0, 0)),
        pl.BlockSpec((n, 2048), lambda k: (0, k)),
        pl.BlockSpec((n, 2048), lambda k: (0, k)),
    ]
    if sums is not None:
        args.append(sums)
        specs.append(pl.BlockSpec(memory_space=pl.ANY))
    return pl.pallas_call(
        gate_up_kernel,
        grid=(4,),
        in_specs=specs,
        out_specs=pl.BlockSpec((1, 512, 512), lambda k: (half, 0, 0)),
        out_shape=jax.ShapeDtypeStruct((2, 512, 512), F32),
        input_output_aliases={} if sums is None else {3: 0},
        compiler_params=params(),
        cost_estimate=pl.CostEstimate(
            flops=1024 * 8192 * 512, bytes_accessed=16 << 20, transcendentals=0
        ),
        name="gate_up",
    )(*args)


def hidden_kernel(
    place, a_ref, q_ref, m_ref, low_ref, ge_ref, ue_ref, de_ref, h_ref, t_ref
):
    low = jnp.dot(q_ref[...], low_ref[...], preferred_element_type=F32)
    lg = low[:, :64].astype(BF)
    lu = low[:, 64:].astype(BF)
    lg = jnp.concatenate([lg] * 4, axis=1)
    lu = jnp.concatenate([lu] * 4, axis=1)
    n = ge_ref.shape[1]
    gate = a_ref[0, :, :n]
    up = a_ref[0, :, 256 : 256 + n]
    for j in range(8):
        mask = m_ref[:, 256 * j : 256 * (j + 1)]
        gate += jnp.dot(lg * mask, ge_ref[pl.ds(256 * j, 256)], preferred_element_type=F32)
        up += jnp.dot(lu * mask, ue_ref[pl.ds(256 * j, 256)], preferred_element_type=F32)
    hidden = (gate / (1.0 + jnp.exp(-gate)) * up).astype(BF)
    down = jnp.zeros((256, 256), F32)
    for j in range(8):
        mask = m_ref[:, 256 * j : 256 * (j + 1)].astype(F32)
        down += nt(hidden, de_ref[pl.ds(256 * j, 256)]) * mask
    down = (down[:, :128] + down[:, 128:]).astype(BF)
    wide = jnp.concatenate([hidden, jnp.zeros((256, 256 - hidden.shape[1]), BF), down], axis=1)
    ry = place[pl.program_id(0)]
    for z in range(4):
        rz = place[4 + z]
        upper = wide[64 * z : 64 * z + 32]
        lower = wide[64 * z + 32 : 64 * z + 64]
        h_ref[(rz + 3) % 4, 0, ry] = upper
        h_ref[(ry + 3) % 4, 1, rz] = lower
        t_ref[(7 - rz) % 4, 0, (4 - ry) % 4] = upper
        t_ref[(7 - ry) % 4, 1, (4 - rz) % 4] = lower


def hidden_rows(place, sums, pick, mask, low, gate_exit, up_exit, down_entry):
    n = gate_exit.shape[1]
    return pl.pallas_call(
        hidden_kernel,
        grid_spec=pltpu.PrefetchScalarGridSpec(
            num_scalar_prefetch=1,
            grid=(4,),
            in_specs=[
                pl.BlockSpec((1, 256, 512), lambda i, p: (i, 0, 0)),
                pl.BlockSpec((256, 2560), lambda i, p: (i, 0)),
                pl.BlockSpec((256, 2048), lambda i, p: (i, 0)),
                pl.BlockSpec((2560, 128), lambda i, p: (0, 0)),
                pl.BlockSpec((2048, n), lambda i, p: (0, 0)),
                pl.BlockSpec((2048, n), lambda i, p: (0, 0)),
                pl.BlockSpec((2048, n), lambda i, p: (0, 0)),
            ],
            out_specs=[pl.BlockSpec((4, 2, 4, 32, 384), lambda i, p: (0, 0, 0, 0, 0))] * 2,
        ),
        out_shape=[jax.ShapeDtypeStruct((4, 2, 4, 32, 384), BF)] * 2,
        compiler_params=params(),
        cost_estimate=pl.CostEstimate(
            flops=2 * 1024 * 2560 * 512, bytes_accessed=16 << 20, transcendentals=1024 * n
        ),
        name="hidden_rows",
    )(place, sums, pick, mask, low, gate_exit, up_exit, down_entry)


def on_device(
    tokens,
    token_adapter,
    adapter_slot_table,
    gate_matrix,
    up_matrix,
    down_matrix,
    adapter_entry_maps,
    adapter_gate_exit,
    adapter_up_exit,
    adapter_down_entry,
    adapter_down_exit,
):
    units = gate_matrix.shape[1]
    a = lax.axis_index("adapter")
    t = lax.axis_index("tensor")
    y, z, x, c = a // 4, a % 4, t // 2, t % 2
    way = 1 - 2 * c

    every = lax.all_gather(tokens, AXES, axis=0, tiled=False).reshape(16, 8, 64, 1024)
    ids = lax.all_gather(token_adapter, "adapter", axis=0, tiled=True)

    exits = []
    for kept, axes in ((0, "yz"), (1, "zy")):
        held = adapter_down_exit[kept]
        for axis in axes:
            held = [held]
            for _ in range(3):
                held.append(ring(held[-1], axis))
            held = jnp.stack(held)
        exits.append(held.reshape(1024, 1024))
    every, exits = lax.optimization_barrier((every, exits))

    names = jnp.arange(32, dtype=jnp.int32)
    member = ids[:, None] == names[None, :]
    order = jnp.arange(1024, dtype=jnp.int32)
    before = (order[:, None] > order[None, :]).astype(BF)
    earlier = jnp.dot(before, member.astype(BF), preferred_element_type=F32).astype(jnp.int32)
    rank_in = jnp.sum(jnp.where(member, earlier, 0), axis=1)
    slot = jnp.sum(jnp.where(member, adapter_slot_table[None, :], 0), axis=1)
    owner = slot // 2
    row = (slot % 2) * SEGMENT + rank_in
    select = (
        (jnp.where(owner == a, row, -1))[None, :] == jnp.arange(160, dtype=jnp.int32)[:, None]
    ).astype(BF).reshape(2, SEGMENT, 1024)
    relative = ((owner % 4 - z) % 4) * 4 + (owner // 4 - y) % 4
    pick = (
        (relative * 160 + row)[:, None] == jnp.arange(2560, dtype=jnp.int32)[None, :]
    ).astype(BF)
    mask = (slot[:, None] == (jnp.arange(2048, dtype=jnp.int32) // 64)[None, :]).astype(BF)

    def column(r, core):
        at = ((x + r) % 4 * 2 + core) * 1024
        return lax.dynamic_slice(down_matrix, (0, at), (units, 1024))

    turns = (1, 2, 3, 0)
    def columns(turns, core, rows, extra):
        width = 1024 * len(turns)
        if extra:
            out = jnp.pad(jnp.eye(128, dtype=BF), ((rows - 128, 0), (width, 0)))
        else:
            out = jnp.zeros((rows, width), BF)
        for i, r in enumerate(turns):
            out = lax.dynamic_update_slice(out, column(r, core), (0, 1024 * i))
        return out

    theirs = columns(turns, 1 - c, 384, True)
    mine = (columns((1, 2), c, 256, False), columns((3, 0), c, 384, True))

    low_own = low_own_rows(every, adapter_entry_maps, select).reshape(160, 128)
    low = jnp.stack([low_own] + [send(low_own, dy=-d) for d in (1, 2, 3)])
    low = jnp.stack([low] + [send(low, dz=-d) for d in (1, 2, 3)]).reshape(2560, 128)
    sums = None
    for half in range(2):
        sums = gate_up(every, gate_matrix.T, up_matrix.T, half, sums)
    sums = sums.reshape(4, 256, 512)

    quarter = jnp.arange(4, dtype=jnp.int32)
    place = jnp.concatenate([way * (y - quarter) % 4, way * (z - quarter) % 4])
    rows, back = hidden_rows(
        place,
        sums,
        pick,
        mask,
        low,
        adapter_gate_exit.reshape(2048, units),
        adapter_up_exit.reshape(2048, units),
        adapter_down_entry.transpose(0, 2, 1).reshape(2048, units),
    )
    rows = rows.reshape(4, 2, 128, 384)
    back = back.reshape(4, 256, 384)
    first = jnp.dot(back[0], theirs, preferred_element_type=F32).astype(BF)
    back, first = lax.optimization_barrier((back, first))
    rest = jnp.dot(back[1:].reshape(768, 384), theirs, preferred_element_type=F32).astype(BF)
    rest, first_other = lax.optimization_barrier((rest, send(first, dc=1)))
    others = jnp.split(send(rest, dc=1).reshape(3, 2, 128, 4224), 3)
    others = [first_other.reshape(1, 2, 128, 4224)] + others

    axes = (("z", "y"), ("y", "z"))
    spans = ((0, 2048), (2048, 4224))

    def own_part(rows, step, ch, color, lo=0, hi=128):
        h = rows[step, color, lo:hi, : mine[ch].shape[0]]
        part = jnp.dot(h, mine[ch], preferred_element_type=F32)
        return part + others[step][0, color, lo:hi, slice(*spans[ch])].astype(F32)

    chains = [(ch, color) for ch in range(2) for color in range(2)]
    came = {k: own_part(rows, 0, *k).astype(BF) for k in chains}
    rows, came = lax.optimization_barrier((rows, came))
    came = {k: ring(v, axes[k[1]][0]) for k, v in came.items()}
    for step in range(1, 3):
        for ch, color in chains:
            total = own_part(rows, step, ch, color) + came[ch, color].astype(F32)
            came[ch, color] = ring(total.astype(BF), axes[color][0])
    summed = []
    for color in range(2):
        parts = {}
        for r in turns:
            lo, hi = 32 * r, 32 * r + 32
            parts[r] = jnp.concatenate(
                [
                    own_part(rows, 3, ch, color, lo, hi) + came[ch, color][lo:hi].astype(F32)
                    for ch in range(2)
                ],
                axis=1,
            )
        total = parts[0]
        for r in (1, 2, 3):
            total += onward(parts[r].astype(BF), axes[color][1], -r).astype(F32)
        summed.append(total)
    summed = jnp.concatenate(summed)
    summed = (summed[:, :2048], summed[:, 2048:])
    tail = summed[1][:, 2048:]
    blocks = {
        1: summed[0][:, :1024],
        2: summed[0][:, 1024:],
        3: summed[1][:, :1024],
        0: summed[1][:, 1024:2048],
    }
    total = jnp.concatenate([blocks[0], tail], axis=1)
    for r in (1, 2, 3):
        total = total + send(
            jnp.concatenate([blocks[r], tail], axis=1).astype(BF), dx=r
        ).astype(F32)

    own_slot = jnp.sum(
        jnp.where(token_adapter[:, None] == names[None, :], adapter_slot_table[None, :], 0), axis=1
    )
    low_down = total[:, 1024:].astype(BF)
    ry = way * (y - own_slot // 8) % 4
    rz = way * (z - own_slot // 2 % 4) % 4
    at = jnp.arange(1024, dtype=jnp.int32) // 64
    result = total[:, :1024]
    for kept, relative in enumerate((rz * 4 + ry, ry * 4 + rz)):
        spread = jnp.tile(low_down[:, 64 * kept : 64 * kept + 64], (1, 16))
        spread = jnp.where(relative[:, None] == at[None, :], spread, 0)
        result += jnp.dot(spread, exits[kept], preferred_element_type=F32)
    return result.astype(BF)


def solution(mesh):
    return jax.shard_map(
        on_device,
        mesh=mesh,
        in_specs=(
            P("adapter", "tensor"),
            P("adapter"),
            P(),
            P(None, ("adapter", "tensor")),
            P(None, ("adapter", "tensor")),
            P(("adapter", "tensor"), None),
            P("adapter", None, None),
            P(None, None, ("adapter", "tensor")),
            P(None, None, ("adapter", "tensor")),
            P(None, ("adapter", "tensor"), None),
            P("adapter", None, "tensor"),
        ),
        out_specs=P("adapter", "tensor"),
        check_vma=False,
    )
```

```python
import functools

import jax
import jax.numpy as jnp
from jax import lax
from jax.experimental import pallas as pl
from jax.experimental.pallas import tpu as pltpu
from jax.sharding import PartitionSpec as P

SEGMENT = 80
BF = jnp.bfloat16
F32 = jnp.float32
AXES = ("adapter", "tensor")
VMEM_LIMIT = 60 * 1024 * 1024


def pairs(move):
    out = []
    for i in range(128):
        y, z, x, c = i // 32, (i // 8) % 4, (i // 2) % 4, i % 2
        ty, tz, tx, tc = move(y, z, x, c)
        out.append((i, (ty % 4) * 32 + (tz % 4) * 8 + (tx % 4) * 2 + tc % 2))
    return out


def send(value, dy=0, dz=0, dx=0, dc=0):
    return lax.ppermute(value, AXES, pairs(lambda y, z, x, c: (y + dy, z + dz, x + dx, c + dc)))


def onward(value, axis, step):
    def move(y, z, x, c):
        d = step * (1 - 2 * c)
        return (y + d, z, x, c) if axis == "y" else (y, z + d, x, c)

    return lax.ppermute(value, AXES, pairs(move))


def ring(value, axis):
    return onward(value, axis, 1)


def params(n=1):
    return pltpu.CompilerParams(
        dimension_semantics=("arbitrary",) * n, vmem_limit_bytes=VMEM_LIMIT
    )


def nt(a, b):
    return lax.dot_general(a, b, (((1,), (1,)), ((), ())), preferred_element_type=F32)


def low_kernel(x_ref, e_ref, s_ref, o_ref, acc):
    k = pl.program_id(0)

    @pl.when(k == 0)
    def _():
        acc[...] = jnp.zeros_like(acc)

    for j in range(2):
        x = x_ref[:, j].reshape(1024, 1024)
        at = pl.ds(1024 * j, 1024)
        e = jnp.concatenate([e_ref[0, at], e_ref[1, at]], axis=1)
        acc[...] += jnp.dot(x, e, preferred_element_type=F32)

    @pl.when(k == pl.num_programs(0) - 1)
    def _():
        for j in range(2):
            o_ref[j] = jnp.dot(
                s_ref[j], acc[:, 128 * j : 128 * (j + 1)].astype(BF), preferred_element_type=F32
            ).astype(BF)


def low_own_rows(every, entry, select):
    return pl.pallas_call(
        low_kernel,
        grid=(4,),
        in_specs=[
            pl.BlockSpec((16, 2, 64, 1024), lambda k: (0, k, 0, 0)),
            pl.BlockSpec((2, 2048, 128), lambda k: (0, k, 0)),
            pl.BlockSpec((2, SEGMENT, 1024), lambda k: (0, 0, 0)),
        ],
        out_specs=pl.BlockSpec((2, SEGMENT, 128), lambda k: (0, 0, 0)),
        out_shape=jax.ShapeDtypeStruct((2, SEGMENT, 128), BF),
        scratch_shapes=[pltpu.VMEM((1024, 256), F32)],
        compiler_params=params(),
        cost_estimate=pl.CostEstimate(
            flops=2 * 1024 * 8192 * 256, bytes_accessed=21 << 20, transcendentals=0
        ),
        name="low_own",
    )(every, entry, select)


def gate_up_kernel(x_ref, g_ref, u_ref, *refs):
    o_ref = refs[-1]
    n = g_ref.shape[0]

    @pl.when(pl.program_id(0) == 0)
    def _():
        o_ref[...] = jnp.zeros_like(o_ref)

    for j in range(2):
        x = x_ref[:, j].reshape(512, 1024)
        at = pl.ds(1024 * j, 1024)
        o_ref[0, :, :n] += nt(x, g_ref[:, at])
        o_ref[0, :, 256 : 256 + n] += nt(x, u_ref[:, at])


def gate_up(every, gate, up, half, sums):
    n = gate.shape[0]
    args = [every, gate, up]
    specs = [
        pl.BlockSpec((8, 2, 64, 1024), lambda k: (half, k, 0, 0)),
        pl.BlockSpec((n, 2048), lambda k: (0, k)),
        pl.BlockSpec((n, 2048), lambda k: (0, k)),
    ]
    if sums is not None:
        args.append(sums)
        specs.append(pl.BlockSpec(memory_space=pl.ANY))
    return pl.pallas_call(
        gate_up_kernel,
        grid=(4,),
        in_specs=specs,
        out_specs=pl.BlockSpec((1, 512, 512), lambda k: (half, 0, 0)),
        out_shape=jax.ShapeDtypeStruct((2, 512, 512), F32),
        input_output_aliases={} if sums is None else {3: 0},
        compiler_params=params(),
        cost_estimate=pl.CostEstimate(
            flops=1024 * 8192 * 512, bytes_accessed=16 << 20, transcendentals=0
        ),
        name="gate_up",
    )(*args)


def hidden_kernel(
    place, a_ref, slot_ref, row_ref, low_ref, ge_ref, ue_ref, de_ref, h_ref, t_ref
):
    lane = lax.broadcasted_iota(jnp.int32, (256, 256), 1)
    row = row_ref[...]
    slot = slot_ref[...]

    def equal(value, index):
        return jnp.where(value == index, 1.0, 0.0)

    low = jnp.zeros((256, 128), F32)
    for j in range(10):
        pick = equal(row, lane + 256 * j).astype(BF)
        low += jnp.dot(pick, low_ref[pl.ds(256 * j, 256)], preferred_element_type=F32)
    lg = low[:, :64].astype(BF)
    lu = low[:, 64:].astype(BF)
    lg = jnp.concatenate([lg] * 4, axis=1)
    lu = jnp.concatenate([lu] * 4, axis=1)
    n = ge_ref.shape[1]
    gate = a_ref[0, :, :n]
    up = a_ref[0, :, 256 : 256 + n]
    for j in range(8):
        mask = equal(slot, lane // 64 + 4 * j).astype(BF)
        gate += jnp.dot(lg * mask, ge_ref[pl.ds(256 * j, 256)], preferred_element_type=F32)
        up += jnp.dot(lu * mask, ue_ref[pl.ds(256 * j, 256)], preferred_element_type=F32)
    hidden = (gate / (1.0 + jnp.exp(-gate)) * up).astype(BF)
    down = jnp.zeros((256, 256), F32)
    for j in range(8):
        mask = equal(slot, lane // 64 + 4 * j)
        down += nt(hidden, de_ref[pl.ds(256 * j, 256)]) * mask
    down = (down[:, :128] + down[:, 128:]).astype(BF)
    wide = jnp.concatenate([hidden, jnp.zeros((256, 256 - hidden.shape[1]), BF), down], axis=1)
    ry = place[pl.program_id(0)]
    for z in range(4):
        rz = place[4 + z]
        upper = wide[64 * z : 64 * z + 32]
        lower = wide[64 * z + 32 : 64 * z + 64]
        h_ref[(rz + 3) % 4, 0, ry] = upper
        h_ref[(ry + 3) % 4, 1, rz] = lower
        t_ref[(7 - rz) % 4, 0, (4 - ry) % 4] = upper
        t_ref[(7 - ry) % 4, 1, (4 - rz) % 4] = lower


def hidden_rows(place, sums, slot, row, low, gate_exit, up_exit, down_entry):
    n = gate_exit.shape[1]
    return pl.pallas_call(
        hidden_kernel,
        grid_spec=pltpu.PrefetchScalarGridSpec(
            num_scalar_prefetch=1,
            grid=(4,),
            in_specs=[
                pl.BlockSpec((1, 256, 512), lambda i, p: (i, 0, 0)),
                pl.BlockSpec((256, 1), lambda i, p: (i, 0)),
                pl.BlockSpec((256, 1), lambda i, p: (i, 0)),
                pl.BlockSpec((2560, 128), lambda i, p: (0, 0)),
                pl.BlockSpec((2048, n), lambda i, p: (0, 0)),
                pl.BlockSpec((2048, n), lambda i, p: (0, 0)),
                pl.BlockSpec((2048, n), lambda i, p: (0, 0)),
            ],
            out_specs=[pl.BlockSpec((4, 2, 4, 32, 384), lambda i, p: (0, 0, 0, 0, 0))] * 2,
        ),
        out_shape=[jax.ShapeDtypeStruct((4, 2, 4, 32, 384), BF)] * 2,
        compiler_params=params(),
        cost_estimate=pl.CostEstimate(
            flops=2 * 1024 * 2560 * 512, bytes_accessed=16 << 20, transcendentals=1024 * n
        ),
        name="hidden_rows",
    )(place, sums, slot, row, low, gate_exit, up_exit, down_entry)


def on_device(
    tokens,
    token_adapter,
    adapter_slot_table,
    gate_matrix,
    up_matrix,
    down_matrix,
    adapter_entry_maps,
    adapter_gate_exit,
    adapter_up_exit,
    adapter_down_entry,
    adapter_down_exit,
):
    units = gate_matrix.shape[1]
    a = lax.axis_index("adapter")
    t = lax.axis_index("tensor")
    y, z, x, c = a // 4, a % 4, t // 2, t % 2
    way = 1 - 2 * c

    every = lax.all_gather(tokens, AXES, axis=0, tiled=False).reshape(16, 8, 64, 1024)
    ids = lax.all_gather(token_adapter, "adapter", axis=0, tiled=True)

    exits = adapter_down_exit
    for axis in "yz":
        exits = [exits]
        for _ in range(3):
            exits.append(ring(exits[-1], axis))
        exits = jnp.stack(exits)
    exits = exits.reshape(2048, 1024)

    names = jnp.arange(32, dtype=jnp.int32)
    member = ids[:, None] == names[None, :]
    order = jnp.arange(1024, dtype=jnp.int32)
    before = (order[:, None] > order[None, :]).astype(BF)
    earlier = jnp.dot(before, member.astype(BF), preferred_element_type=F32).astype(jnp.int32)
    rank_in = jnp.sum(jnp.where(member, earlier, 0), axis=1)
    slot = jnp.sum(jnp.where(member, adapter_slot_table[None, :], 0), axis=1)
    owner = slot // 2
    row = (slot % 2) * SEGMENT + rank_in
    select = (
        (jnp.where(owner == a, row, -1))[None, :] == jnp.arange(160, dtype=jnp.int32)[:, None]
    ).astype(BF).reshape(2, SEGMENT, 1024)
    relative = ((owner % 4 - z) % 4) * 4 + (owner // 4 - y) % 4

    def column(r, core):
        at = ((x + r) % 4 * 2 + core) * 1024
        return lax.dynamic_slice(down_matrix, (0, at), (units, 1024))

    turns = (1, 2, 3, 0)
    def columns(turns, core, rows, extra):
        width = 1024 * len(turns)
        if extra:
            out = jnp.pad(jnp.eye(128, dtype=BF), ((rows - 128, 0), (width, 0)))
        else:
            out = jnp.zeros((rows, width), BF)
        for i, r in enumerate(turns):
            out = lax.dynamic_update_slice(out, column(r, core), (0, 1024 * i))
        return out

    theirs = columns(turns, 1 - c, 384, True)
    mine = (columns((1, 2), c, 256, False), columns((3, 0), c, 384, True))

    every, exits, select, slot, row, theirs, mine = lax.optimization_barrier(
        (every, exits, select, slot, (relative * 160 + row)[:, None], theirs, mine)
    )
    low_own = low_own_rows(every, adapter_entry_maps, select).reshape(160, 128)
    low = jnp.stack([low_own] + [send(low_own, dy=-d) for d in (1, 2, 3)])
    low = jnp.stack([low] + [send(low, dz=-d) for d in (1, 2, 3)]).reshape(2560, 128)
    sums = None
    for half in range(2):
        sums = gate_up(every, gate_matrix.T, up_matrix.T, half, sums)
    sums = sums.reshape(4, 256, 512)

    quarter = jnp.arange(4, dtype=jnp.int32)
    place = jnp.concatenate([way * (y - quarter) % 4, way * (z - quarter) % 4])
    rows, back = hidden_rows(
        place,
        sums,
        slot[:, None],
        row,
        low,
        adapter_gate_exit.reshape(2048, units),
        adapter_up_exit.reshape(2048, units),
        adapter_down_entry.transpose(0, 2, 1).reshape(2048, units),
    )
    rows = rows.reshape(4, 2, 128, 384)
    back = back.reshape(4, 256, 384)
    first = jnp.dot(back[0], theirs, preferred_element_type=F32).astype(BF)
    back, first = lax.optimization_barrier((back, first))
    rest = jnp.dot(back[1:].reshape(768, 384), theirs, preferred_element_type=F32).astype(BF)
    rest, first_other = lax.optimization_barrier((rest, send(first, dc=1)))
    others = jnp.split(send(rest, dc=1).reshape(3, 2, 128, 4224), 3)
    others = [first_other.reshape(1, 2, 128, 4224)] + others

    axes = (("z", "y"), ("y", "z"))
    spans = ((0, 2048), (2048, 4224))

    def own_part(rows, step, ch, color, lo=0, hi=128):
        h = rows[step, color, lo:hi, : mine[ch].shape[0]]
        part = jnp.dot(h, mine[ch], preferred_element_type=F32)
        return part + others[step][0, color, lo:hi, slice(*spans[ch])].astype(F32)

    chains = [(ch, color) for ch in range(2) for color in range(2)]
    came = {k: own_part(rows, 0, *k).astype(BF) for k in chains}
    rows, came = lax.optimization_barrier((rows, came))
    came = {k: ring(v, axes[k[1]][0]) for k, v in came.items()}
    for step in range(1, 3):
        for ch, color in chains:
            total = own_part(rows, step, ch, color) + came[ch, color].astype(F32)
            came[ch, color] = ring(total.astype(BF), axes[color][0])
    summed = []
    for color in range(2):
        parts = {}
        for r in turns:
            lo, hi = 32 * r, 32 * r + 32
            parts[r] = jnp.concatenate(
                [
                    own_part(rows, 3, ch, color, lo, hi) + came[ch, color][lo:hi].astype(F32)
                    for ch in range(2)
                ],
                axis=1,
            )
        total = parts[0]
        for r in (1, 2, 3):
            total += onward(parts[r].astype(BF), axes[color][1], -r).astype(F32)
        summed.append(total)
    summed = jnp.concatenate(summed)
    summed = (summed[:, :2048], summed[:, 2048:])
    tail = summed[1][:, 2048:]
    blocks = {
        1: summed[0][:, :1024],
        2: summed[0][:, 1024:],
        3: summed[1][:, :1024],
        0: summed[1][:, 1024:2048],
    }
    total = jnp.concatenate([blocks[0], tail], axis=1)
    for r in (1, 2, 3):
        total = total + send(
            jnp.concatenate([blocks[r], tail], axis=1).astype(BF), dx=r
        ).astype(F32)

    own_slot = jnp.sum(
        jnp.where(token_adapter[:, None] == names[None, :], adapter_slot_table[None, :], 0), axis=1
    )
    low_down = total[:, 1024:].astype(BF)
    ry = way * (y - own_slot // 8) % 4
    rz = way * (z - own_slot // 2 % 4) % 4
    at = jnp.arange(2048, dtype=jnp.int32) // 128
    spread = jnp.where((rz * 4 + ry)[:, None] == at[None, :], jnp.tile(low_down, (1, 16)), 0)
    delta = jnp.dot(spread, exits, preferred_element_type=F32)
    return (total[:, :1024] + delta).astype(BF)


def solution(mesh):
    return jax.shard_map(
        on_device,
        mesh=mesh,
        in_specs=(
            P("adapter", "tensor"),
            P("adapter"),
            P(),
            P(None, ("adapter", "tensor")),
            P(None, ("adapter", "tensor")),
            P(("adapter", "tensor"), None),
            P("adapter", None, None),
            P(None, None, ("adapter", "tensor")),
            P(None, None, ("adapter", "tensor")),
            P(None, ("adapter", "tensor"), None),
            P("adapter", None, "tensor"),
        ),
        out_specs=P("adapter", "tensor"),
        check_vma=False,
    )
```

```python
import functools

import jax
import jax.numpy as jnp
from jax import lax
from jax.experimental import pallas as pl
from jax.experimental.pallas import tpu as pltpu
from jax.sharding import PartitionSpec as P

SEGMENT = 80
BF = jnp.bfloat16
F32 = jnp.float32
AXES = ("adapter", "tensor")
VMEM_LIMIT = 60 * 1024 * 1024


def pairs(move):
    out = []
    for i in range(128):
        y, z, x, c = i // 32, (i // 8) % 4, (i // 2) % 4, i % 2
        ty, tz, tx, tc = move(y, z, x, c)
        out.append((i, (ty % 4) * 32 + (tz % 4) * 8 + (tx % 4) * 2 + tc % 2))
    return out


def send(value, dy=0, dz=0, dx=0, dc=0):
    return lax.ppermute(value, AXES, pairs(lambda y, z, x, c: (y + dy, z + dz, x + dx, c + dc)))


def onward(value, axis, step):
    def move(y, z, x, c):
        d = step * (1 - 2 * c)
        return (y + d, z, x, c) if axis == "y" else (y, z + d, x, c)

    return lax.ppermute(value, AXES, pairs(move))


def ring(value, axis):
    return onward(value, axis, 1)


def params(n=1):
    return pltpu.CompilerParams(
        dimension_semantics=("arbitrary",) * n, vmem_limit_bytes=VMEM_LIMIT
    )


def nt(a, b):
    return lax.dot_general(a, b, (((1,), (1,)), ((), ())), preferred_element_type=F32)


def low_kernel(x_ref, e_ref, s_ref, o_ref, acc):
    k = pl.program_id(0)

    @pl.when(k == 0)
    def _():
        acc[...] = jnp.zeros_like(acc)

    for j in range(2):
        x = x_ref[:, j].reshape(1024, 1024)
        at = pl.ds(1024 * j, 1024)
        e = jnp.concatenate([e_ref[0, at], e_ref[1, at]], axis=1)
        acc[...] += jnp.dot(x, e, preferred_element_type=F32)

    @pl.when(k == pl.num_programs(0) - 1)
    def _():
        for j in range(2):
            o_ref[j] = jnp.dot(
                s_ref[j], acc[:, 128 * j : 128 * (j + 1)].astype(BF), preferred_element_type=F32
            ).astype(BF)


def low_own_rows(every, entry, select):
    return pl.pallas_call(
        low_kernel,
        grid=(4,),
        in_specs=[
            pl.BlockSpec((16, 2, 64, 1024), lambda k: (0, k, 0, 0)),
            pl.BlockSpec((2, 2048, 128), lambda k: (0, k, 0)),
            pl.BlockSpec((2, SEGMENT, 1024), lambda k: (0, 0, 0)),
        ],
        out_specs=pl.BlockSpec((2, SEGMENT, 128), lambda k: (0, 0, 0)),
        out_shape=jax.ShapeDtypeStruct((2, SEGMENT, 128), BF),
        scratch_shapes=[pltpu.VMEM((1024, 256), F32)],
        compiler_params=params(),
        cost_estimate=pl.CostEstimate(
            flops=2 * 1024 * 8192 * 256, bytes_accessed=21 << 20, transcendentals=0
        ),
        name="low_own",
    )(every, entry, select)


def gate_up_kernel(x_ref, g_ref, u_ref, *refs):
    o_ref = refs[-1]
    n = g_ref.shape[0]

    @pl.when(pl.program_id(0) == 0)
    def _():
        o_ref[...] = jnp.zeros_like(o_ref)

    for j in range(2):
        x = x_ref[:, j].reshape(512, 1024)
        at = pl.ds(1024 * j, 1024)
        o_ref[0, :, :n] += nt(x, g_ref[:, at])
        o_ref[0, :, 256 : 256 + n] += nt(x, u_ref[:, at])


def gate_up(every, gate, up, half, sums):
    n = gate.shape[0]
    args = [every, gate, up]
    specs = [
        pl.BlockSpec((8, 2, 64, 1024), lambda k: (half, k, 0, 0)),
        pl.BlockSpec((n, 2048), lambda k: (0, k)),
        pl.BlockSpec((n, 2048), lambda k: (0, k)),
    ]
    if sums is not None:
        args.append(sums)
        specs.append(pl.BlockSpec(memory_space=pl.ANY))
    return pl.pallas_call(
        gate_up_kernel,
        grid=(4,),
        in_specs=specs,
        out_specs=pl.BlockSpec((1, 512, 512), lambda k: (half, 0, 0)),
        out_shape=jax.ShapeDtypeStruct((2, 512, 512), F32),
        input_output_aliases={} if sums is None else {3: 0},
        compiler_params=params(),
        cost_estimate=pl.CostEstimate(
            flops=1024 * 8192 * 512, bytes_accessed=16 << 20, transcendentals=0
        ),
        name="gate_up",
    )(*args)


def hidden_kernel(
    place, a_ref, slot_ref, row_ref, low_ref, ge_ref, ue_ref, de_ref, h_ref, t_ref
):
    lane = lax.broadcasted_iota(jnp.int32, (512, 256), 1)
    row = row_ref[...]
    slot = slot_ref[...]

    def equal(value, index):
        return jnp.where(value == index, 1.0, 0.0)

    low = jnp.zeros((512, 128), F32)
    for j in range(10):
        pick = equal(row, lane + 256 * j).astype(BF)
        low += jnp.dot(pick, low_ref[pl.ds(256 * j, 256)], preferred_element_type=F32)
    lg = low[:, :64].astype(BF)
    lu = low[:, 64:].astype(BF)
    lg = jnp.concatenate([lg] * 4, axis=1)
    lu = jnp.concatenate([lu] * 4, axis=1)
    n = ge_ref.shape[1]
    gate = a_ref[0, :, :n]
    up = a_ref[0, :, 256 : 256 + n]
    for j in range(8):
        mask = equal(slot, lane // 64 + 4 * j).astype(BF)
        gate += jnp.dot(lg * mask, ge_ref[pl.ds(256 * j, 256)], preferred_element_type=F32)
        up += jnp.dot(lu * mask, ue_ref[pl.ds(256 * j, 256)], preferred_element_type=F32)
    hidden = (gate / (1.0 + jnp.exp(-gate)) * up).astype(BF)
    down = jnp.zeros((512, 256), F32)
    for j in range(8):
        mask = equal(slot, lane // 64 + 4 * j)
        down += nt(hidden, de_ref[pl.ds(256 * j, 256)]) * mask
    down = (down[:, :128] + down[:, 128:]).astype(BF)
    wide = jnp.concatenate([hidden, jnp.zeros((512, 256 - hidden.shape[1]), BF), down], axis=1)
    for y in range(2):
        ry = place[2 * pl.program_id(0) + y]
        for z in range(4):
            rz = place[4 + z]
            at = 256 * y + 64 * z
            upper = wide[at : at + 32]
            lower = wide[at + 32 : at + 64]
            h_ref[(rz + 3) % 4, 0, ry] = upper
            h_ref[(ry + 3) % 4, 1, rz] = lower
            t_ref[(7 - rz) % 4, 0, (4 - ry) % 4] = upper
            t_ref[(7 - ry) % 4, 1, (4 - rz) % 4] = lower


def hidden_rows(place, sums, slot, row, low, gate_exit, up_exit, down_entry):
    n = gate_exit.shape[1]
    return pl.pallas_call(
        hidden_kernel,
        grid_spec=pltpu.PrefetchScalarGridSpec(
            num_scalar_prefetch=1,
            grid=(2,),
            in_specs=[
                pl.BlockSpec((1, 512, 512), lambda i, p: (i, 0, 0)),
                pl.BlockSpec((512, 1), lambda i, p: (i, 0)),
                pl.BlockSpec((512, 1), lambda i, p: (i, 0)),
                pl.BlockSpec((2560, 128), lambda i, p: (0, 0)),
                pl.BlockSpec((2048, n), lambda i, p: (0, 0)),
                pl.BlockSpec((2048, n), lambda i, p: (0, 0)),
                pl.BlockSpec((2048, n), lambda i, p: (0, 0)),
            ],
            out_specs=[pl.BlockSpec((4, 2, 4, 32, 384), lambda i, p: (0, 0, 0, 0, 0))] * 2,
        ),
        out_shape=[jax.ShapeDtypeStruct((4, 2, 4, 32, 384), BF)] * 2,
        compiler_params=params(),
        cost_estimate=pl.CostEstimate(
            flops=2 * 1024 * 2560 * 512, bytes_accessed=16 << 20, transcendentals=1024 * n
        ),
        name="hidden_rows",
    )(place, sums, slot, row, low, gate_exit, up_exit, down_entry)


def on_device(
    tokens,
    token_adapter,
    adapter_slot_table,
    gate_matrix,
    up_matrix,
    down_matrix,
    adapter_entry_maps,
    adapter_gate_exit,
    adapter_up_exit,
    adapter_down_entry,
    adapter_down_exit,
):
    units = gate_matrix.shape[1]
    a = lax.axis_index("adapter")
    t = lax.axis_index("tensor")
    y, z, x, c = a // 4, a % 4, t // 2, t % 2
    way = 1 - 2 * c

    every = lax.all_gather(tokens, AXES, axis=0, tiled=False).reshape(16, 8, 64, 1024)
    kept = jnp.concatenate(
        [
            adapter_down_exit.reshape(128, 1024),
            jnp.pad(token_adapter.astype(BF)[None, :], ((0, 7), (0, 960))),
        ]
    )
    for axis in "yz":
        kept = [kept]
        for _ in range(3):
            kept.append(ring(kept[-1], axis))
        if axis == "y":
            kept = jnp.stack(kept)
    quarter = jnp.arange(4, dtype=jnp.int32)
    homes = ((z - way * quarter) % 4)[:, None] + ((y - way * quarter) % 4 * 4)[None, :]
    ids = jnp.stack([v[:, 128, :64] for v in kept]).reshape(16, 64).astype(jnp.int32)
    home = jnp.arange(16, dtype=jnp.int32)[:, None] == homes.reshape(1, 16)
    ids = jnp.sum(jnp.where(home[:, :, None], ids[None], 0), axis=1).reshape(1024)

    names = jnp.arange(32, dtype=jnp.int32)
    member = ids[:, None] == names[None, :]
    order = jnp.arange(1024, dtype=jnp.int32)
    before = (order[:, None] > order[None, :]).astype(BF)
    earlier = jnp.dot(before, member.astype(BF), preferred_element_type=F32).astype(jnp.int32)
    rank_in = jnp.sum(jnp.where(member, earlier, 0), axis=1)
    slot = jnp.sum(jnp.where(member, adapter_slot_table[None, :], 0), axis=1)
    owner = slot // 2
    row = (slot % 2) * SEGMENT + rank_in
    select = (
        (jnp.where(owner == a, row, -1))[None, :] == jnp.arange(160, dtype=jnp.int32)[:, None]
    ).astype(BF).reshape(2, SEGMENT, 1024)
    relative = ((owner % 4 - z) % 4) * 4 + (owner // 4 - y) % 4

    def column(r, core):
        at = ((x + r) % 4 * 2 + core) * 1024
        return lax.dynamic_slice(down_matrix, (0, at), (units, 1024))

    turns = (1, 2, 3, 0)
    def columns(turns, core, rows, extra):
        width = 1024 * len(turns)
        if extra:
            out = jnp.pad(jnp.eye(128, dtype=BF), ((rows - 128, 0), (width, 0)))
        else:
            out = jnp.zeros((rows, width), BF)
        for i, r in enumerate(turns):
            out = lax.dynamic_update_slice(out, column(r, core), (0, 1024 * i))
        return out

    theirs = columns(turns, 1 - c, 384, True)
    mine = (columns((1, 2), c, 256, False), columns((3, 0), c, 384, True))

    every, kept, select, slot, row, theirs, mine = lax.optimization_barrier(
        (every, kept, select, slot, (relative * 160 + row)[:, None], theirs, mine)
    )
    low_own = low_own_rows(every, adapter_entry_maps, select).reshape(160, 128)
    gates = (gate_matrix.T, up_matrix.T)
    low = jnp.stack([low_own] + [send(low_own, dy=-d) for d in (1, 2, 3)])
    sums = gate_up(every, *gates, 0, None)
    low, sums = lax.optimization_barrier((low, sums))
    low = jnp.stack([low] + [send(low, dz=-d) for d in (1, 2, 3)]).reshape(2560, 128)
    sums = gate_up(every, *gates, 1, sums)

    place = jnp.concatenate([way * (y - quarter) % 4, way * (z - quarter) % 4])
    rows, back = hidden_rows(
        place,
        sums,
        slot[:, None],
        row,
        low,
        adapter_gate_exit.reshape(2048, units),
        adapter_up_exit.reshape(2048, units),
        adapter_down_entry.transpose(0, 2, 1).reshape(2048, units),
    )
    rows = rows.reshape(4, 2, 128, 384)
    back = back.reshape(4, 256, 384)
    first = jnp.dot(back[0], theirs, preferred_element_type=F32).astype(BF)
    back, first = lax.optimization_barrier((back, first))
    rest = jnp.dot(back[1:].reshape(768, 384), theirs, preferred_element_type=F32).astype(BF)
    rest, first_other = lax.optimization_barrier((rest, send(first, dc=1)))
    others = jnp.split(send(rest, dc=1).reshape(3, 2, 128, 4224), 3)
    others = [first_other.reshape(1, 2, 128, 4224)] + others

    axes = (("z", "y"), ("y", "z"))
    spans = ((0, 2048), (2048, 4224))

    def own_part(rows, step, ch, color, lo=0, hi=128):
        h = rows[step, color, lo:hi, : mine[ch].shape[0]]
        part = jnp.dot(h, mine[ch], preferred_element_type=F32)
        return part + others[step][0, color, lo:hi, slice(*spans[ch])].astype(F32)

    chains = [(ch, color) for ch in range(2) for color in range(2)]
    came = {k: own_part(rows, 0, *k).astype(BF) for k in chains}
    rows, came, kept = lax.optimization_barrier((rows, came, kept))
    exits = jnp.stack([v[:, :128] for v in kept]).reshape(2048, 1024)
    came = {k: ring(v, axes[k[1]][0]) for k, v in came.items()}
    for step in range(1, 3):
        for ch, color in chains:
            total = own_part(rows, step, ch, color) + came[ch, color].astype(F32)
            came[ch, color] = ring(total.astype(BF), axes[color][0])
        if step == 1:
            came, exits = lax.optimization_barrier((came, exits))
    summed = []
    for color in range(2):
        parts = {}
        for r in turns:
            lo, hi = 32 * r, 32 * r + 32
            parts[r] = jnp.concatenate(
                [
                    own_part(rows, 3, ch, color, lo, hi) + came[ch, color][lo:hi].astype(F32)
                    for ch in range(2)
                ],
                axis=1,
            )
        total = parts[0]
        for r in (1, 2, 3):
            total += onward(parts[r].astype(BF), axes[color][1], -r).astype(F32)
        summed.append(total)
    summed = jnp.concatenate(summed)
    summed = (summed[:, :2048], summed[:, 2048:])
    tail = summed[1][:, 2048:]
    blocks = {
        1: summed[0][:, :1024],
        2: summed[0][:, 1024:],
        3: summed[1][:, :1024],
        0: summed[1][:, 1024:2048],
    }
    total = jnp.concatenate([blocks[0], tail], axis=1)
    for r in (1, 2, 3):
        total = total + send(
            jnp.concatenate([blocks[r], tail], axis=1).astype(BF), dx=r
        ).astype(F32)

    own_slot = jnp.sum(
        jnp.where(token_adapter[:, None] == names[None, :], adapter_slot_table[None, :], 0), axis=1
    )
    low_down = total[:, 1024:].astype(BF)
    ry = way * (y - own_slot // 8) % 4
    rz = way * (z - own_slot // 2 % 4) % 4
    at = jnp.arange(2048, dtype=jnp.int32) // 128
    spread = jnp.where((rz * 4 + ry)[:, None] == at[None, :], jnp.tile(low_down, (1, 16)), 0)
    delta = jnp.dot(spread, exits, preferred_element_type=F32)
    return (total[:, :1024] + delta).astype(BF)


def solution(mesh):
    return jax.shard_map(
        on_device,
        mesh=mesh,
        in_specs=(
            P("adapter", "tensor"),
            P("adapter"),
            P(),
            P(None, ("adapter", "tensor")),
            P(None, ("adapter", "tensor")),
            P(("adapter", "tensor"), None),
            P("adapter", None, None),
            P(None, None, ("adapter", "tensor")),
            P(None, None, ("adapter", "tensor")),
            P(None, ("adapter", "tensor"), None),
            P("adapter", None, "tensor"),
        ),
        out_specs=P("adapter", "tensor"),
        check_vma=False,
    )
```

```python
import functools

import jax
import jax.numpy as jnp
from jax import lax
from jax.experimental import pallas as pl
from jax.experimental.pallas import tpu as pltpu
from jax.sharding import PartitionSpec as P

SEGMENT = 80
BF = jnp.bfloat16
F32 = jnp.float32
AXES = ("adapter", "tensor")
VMEM_LIMIT = 60 * 1024 * 1024


def pairs(move):
    out = []
    for i in range(128):
        y, z, x, c = i // 32, (i // 8) % 4, (i // 2) % 4, i % 2
        ty, tz, tx, tc = move(y, z, x, c)
        out.append((i, (ty % 4) * 32 + (tz % 4) * 8 + (tx % 4) * 2 + tc % 2))
    return out


def send(value, dy=0, dz=0, dx=0, dc=0):
    return lax.ppermute(value, AXES, pairs(lambda y, z, x, c: (y + dy, z + dz, x + dx, c + dc)))


def onward(value, axis, step):
    def move(y, z, x, c):
        d = step * (1 - 2 * c)
        return (y + d, z, x, c) if axis == "y" else (y, z + d, x, c)

    return lax.ppermute(value, AXES, pairs(move))


def ring(value, axis):
    return onward(value, axis, 1)


def params(n=1):
    return pltpu.CompilerParams(
        dimension_semantics=("arbitrary",) * n, vmem_limit_bytes=VMEM_LIMIT
    )


def nt(a, b):
    return lax.dot_general(a, b, (((1,), (1,)), ((), ())), preferred_element_type=F32)


def low_kernel(x_ref, e_ref, s_ref, o_ref, acc):
    k = pl.program_id(0)

    @pl.when(k == 0)
    def _():
        acc[...] = jnp.zeros_like(acc)

    for j in range(2):
        x = x_ref[:, j].reshape(1024, 1024)
        at = pl.ds(1024 * j, 1024)
        e = jnp.concatenate([e_ref[0, at], e_ref[1, at]], axis=1)
        acc[...] += jnp.dot(x, e, preferred_element_type=F32)

    @pl.when(k == pl.num_programs(0) - 1)
    def _():
        for j in range(2):
            o_ref[j] = jnp.dot(
                s_ref[j], acc[:, 128 * j : 128 * (j + 1)].astype(BF), preferred_element_type=F32
            ).astype(BF)


def low_own_rows(every, entry, select):
    return pl.pallas_call(
        low_kernel,
        grid=(4,),
        in_specs=[
            pl.BlockSpec((16, 2, 64, 1024), lambda k: (0, k, 0, 0)),
            pl.BlockSpec((2, 2048, 128), lambda k: (0, k, 0)),
            pl.BlockSpec((2, SEGMENT, 1024), lambda k: (0, 0, 0)),
        ],
        out_specs=pl.BlockSpec((2, SEGMENT, 128), lambda k: (0, 0, 0)),
        out_shape=jax.ShapeDtypeStruct((2, SEGMENT, 128), BF),
        scratch_shapes=[pltpu.VMEM((1024, 256), F32)],
        compiler_params=params(),
        cost_estimate=pl.CostEstimate(
            flops=2 * 1024 * 8192 * 256, bytes_accessed=21 << 20, transcendentals=0
        ),
        name="low_own",
    )(every, entry, select)


def gate_up_kernel(x_ref, g_ref, u_ref, *refs):
    o_ref = refs[-1]
    n = g_ref.shape[0]

    @pl.when(pl.program_id(0) == 0)
    def _():
        o_ref[...] = jnp.zeros_like(o_ref)

    for j in range(2):
        x = x_ref[:, j].reshape(512, 1024)
        at = pl.ds(1024 * j, 1024)
        o_ref[0, :, :n] += nt(x, g_ref[:, at])
        o_ref[0, :, 256 : 256 + n] += nt(x, u_ref[:, at])


def gate_up(every, gate, up, half, sums):
    n = gate.shape[0]
    args = [every, gate, up]
    specs = [
        pl.BlockSpec((8, 2, 64, 1024), lambda k: (half, k, 0, 0)),
        pl.BlockSpec((n, 2048), lambda k: (0, k)),
        pl.BlockSpec((n, 2048), lambda k: (0, k)),
    ]
    if sums is not None:
        args.append(sums)
        specs.append(pl.BlockSpec(memory_space=pl.ANY))
    return pl.pallas_call(
        gate_up_kernel,
        grid=(4,),
        in_specs=specs,
        out_specs=pl.BlockSpec((1, 512, 512), lambda k: (half, 0, 0)),
        out_shape=jax.ShapeDtypeStruct((2, 512, 512), F32),
        input_output_aliases={} if sums is None else {3: 0},
        compiler_params=params(),
        cost_estimate=pl.CostEstimate(
            flops=1024 * 8192 * 512, bytes_accessed=16 << 20, transcendentals=0
        ),
        name="gate_up",
    )(*args)


def hidden_kernel(
    place, a_ref, slot_ref, row_ref, low_ref, ge_ref, ue_ref, de_ref, h_ref, t_ref
):
    lane = lax.broadcasted_iota(jnp.int32, (256, 256), 1)
    row = row_ref[...]
    slot = slot_ref[...]

    def equal(value, index):
        return jnp.where(value == index, 1.0, 0.0)

    low = jnp.zeros((256, 128), F32)
    for j in range(10):
        pick = equal(row, lane + 256 * j).astype(BF)
        low += jnp.dot(pick, low_ref[pl.ds(256 * j, 256)], preferred_element_type=F32)
    lg = low[:, :64].astype(BF)
    lu = low[:, 64:].astype(BF)
    lg = jnp.concatenate([lg] * 4, axis=1)
    lu = jnp.concatenate([lu] * 4, axis=1)
    n = ge_ref.shape[1]
    gate = a_ref[0, :, :n]
    up = a_ref[0, :, 256 : 256 + n]
    for j in range(8):
        mask = equal(slot, lane // 64 + 4 * j).astype(BF)
        gate += jnp.dot(lg * mask, ge_ref[pl.ds(256 * j, 256)], preferred_element_type=F32)
        up += jnp.dot(lu * mask, ue_ref[pl.ds(256 * j, 256)], preferred_element_type=F32)
    hidden = (gate / (1.0 + jnp.exp(-gate)) * up).astype(BF)
    down = jnp.zeros((256, 256), F32)
    for j in range(8):
        mask = equal(slot, lane // 64 + 4 * j)
        down += nt(hidden, de_ref[pl.ds(256 * j, 256)]) * mask
    down = (down[:, :128] + down[:, 128:]).astype(BF)
    wide = jnp.concatenate([hidden, jnp.zeros((256, 256 - hidden.shape[1]), BF), down], axis=1)
    ry = place[pl.program_id(0)]
    for z in range(4):
        rz = place[4 + z]
        upper = wide[64 * z : 64 * z + 32]
        lower = wide[64 * z + 32 : 64 * z + 64]
        h_ref[(rz + 3) % 4, 0, ry] = upper
        h_ref[(ry + 3) % 4, 1, rz] = lower
        t_ref[(7 - rz) % 4, 0, (4 - ry) % 4] = upper
        t_ref[(7 - ry) % 4, 1, (4 - rz) % 4] = lower


def hidden_rows(place, sums, slot, row, low, gate_exit, up_exit, down_entry):
    n = gate_exit.shape[1]
    return pl.pallas_call(
        hidden_kernel,
        grid_spec=pltpu.PrefetchScalarGridSpec(
            num_scalar_prefetch=1,
            grid=(4,),
            in_specs=[
                pl.BlockSpec((1, 256, 512), lambda i, p: (i, 0, 0)),
                pl.BlockSpec((256, 1), lambda i, p: (i, 0)),
                pl.BlockSpec((256, 1), lambda i, p: (i, 0)),
                pl.BlockSpec((2560, 128), lambda i, p: (0, 0)),
                pl.BlockSpec((2048, n), lambda i, p: (0, 0)),
                pl.BlockSpec((2048, n), lambda i, p: (0, 0)),
                pl.BlockSpec((2048, n), lambda i, p: (0, 0)),
            ],
            out_specs=[pl.BlockSpec((4, 2, 4, 32, 384), lambda i, p: (0, 0, 0, 0, 0))] * 2,
        ),
        out_shape=[jax.ShapeDtypeStruct((4, 2, 4, 32, 384), BF)] * 2,
        compiler_params=params(),
        cost_estimate=pl.CostEstimate(
            flops=2 * 1024 * 2560 * 512, bytes_accessed=16 << 20, transcendentals=1024 * n
        ),
        name="hidden_rows",
    )(place, sums, slot, row, low, gate_exit, up_exit, down_entry)


def on_device(
    tokens,
    token_adapter,
    adapter_slot_table,
    gate_matrix,
    up_matrix,
    down_matrix,
    adapter_entry_maps,
    adapter_gate_exit,
    adapter_up_exit,
    adapter_down_entry,
    adapter_down_exit,
):
    units = gate_matrix.shape[1]
    a = lax.axis_index("adapter")
    t = lax.axis_index("tensor")
    y, z, x, c = a // 4, a % 4, t // 2, t % 2
    way = 1 - 2 * c

    every = lax.all_gather(tokens, AXES, axis=0, tiled=False).reshape(16, 8, 64, 1024)
    ids = lax.all_gather(token_adapter, "adapter", axis=0, tiled=True)

    exits = adapter_down_exit
    for axis in "yz":
        exits = [exits]
        for _ in range(3):
            exits.append(ring(exits[-1], axis))
        if axis == "y":
            exits, ids = lax.optimization_barrier((jnp.stack(exits), ids))

    names = jnp.arange(32, dtype=jnp.int32)
    member = ids[:, None] == names[None, :]
    order = jnp.arange(1024, dtype=jnp.int32)
    before = (order[:, None] > order[None, :]).astype(BF)
    earlier = jnp.dot(before, member.astype(BF), preferred_element_type=F32).astype(jnp.int32)
    rank_in = jnp.sum(jnp.where(member, earlier, 0), axis=1)
    slot = jnp.sum(jnp.where(member, adapter_slot_table[None, :], 0), axis=1)
    owner = slot // 2
    row = (slot % 2) * SEGMENT + rank_in
    select = (
        (jnp.where(owner == a, row, -1))[None, :] == jnp.arange(160, dtype=jnp.int32)[:, None]
    ).astype(BF).reshape(2, SEGMENT, 1024)
    relative = ((owner % 4 - z) % 4) * 4 + (owner // 4 - y) % 4

    def column(r, core):
        at = ((x + r) % 4 * 2 + core) * 1024
        return lax.dynamic_slice(down_matrix, (0, at), (units, 1024))

    turns = (1, 2, 3, 0)
    def columns(turns, core, rows, extra):
        width = 1024 * len(turns)
        if extra:
            out = jnp.pad(jnp.eye(128, dtype=BF), ((rows - 128, 0), (width, 0)))
        else:
            out = jnp.zeros((rows, width), BF)
        for i, r in enumerate(turns):
            out = lax.dynamic_update_slice(out, column(r, core), (0, 1024 * i))
        return out

    theirs = columns(turns, 1 - c, 384, True)
    mine = (columns((1, 2), c, 256, False), columns((3, 0), c, 384, True))

    every, select, slot, row, theirs, mine = lax.optimization_barrier(
        (every, select, slot, (relative * 160 + row)[:, None], theirs, mine)
    )
    low_own = low_own_rows(every, adapter_entry_maps, select).reshape(160, 128)
    low_own, exits = lax.optimization_barrier((low_own, exits))
    exits = jnp.stack(exits).reshape(2048, 1024)
    low = jnp.stack([low_own] + [send(low_own, dy=-d) for d in (1, 2, 3)])
    low = jnp.stack([low] + [send(low, dz=-d) for d in (1, 2, 3)]).reshape(2560, 128)
    sums = None
    for half in range(2):
        sums = gate_up(every, gate_matrix.T, up_matrix.T, half, sums)
    sums = sums.reshape(4, 256, 512)

    quarter = jnp.arange(4, dtype=jnp.int32)
    place = jnp.concatenate([way * (y - quarter) % 4, way * (z - quarter) % 4])
    rows, back = hidden_rows(
        place,
        sums,
        slot[:, None],
        row,
        low,
        adapter_gate_exit.reshape(2048, units),
        adapter_up_exit.reshape(2048, units),
        adapter_down_entry.transpose(0, 2, 1).reshape(2048, units),
    )
    rows = rows.reshape(4, 2, 128, 384)
    back = back.reshape(4, 256, 384)
    first = jnp.dot(back[0], theirs, preferred_element_type=F32).astype(BF)
    back, first = lax.optimization_barrier((back, first))
    rest = jnp.dot(back[1:].reshape(768, 384), theirs, preferred_element_type=F32).astype(BF)
    rest, first_other = lax.optimization_barrier((rest, send(first, dc=1)))
    others = jnp.split(send(rest, dc=1).reshape(3, 2, 128, 4224), 3)
    others = [first_other.reshape(1, 2, 128, 4224)] + others

    axes = (("z", "y"), ("y", "z"))
    spans = ((0, 2048), (2048, 4224))

    def own_part(rows, step, ch, color, lo=0, hi=128):
        h = rows[step, color, lo:hi, : mine[ch].shape[0]]
        part = jnp.dot(h, mine[ch], preferred_element_type=F32)
        return part + others[step][0, color, lo:hi, slice(*spans[ch])].astype(F32)

    chains = [(ch, color) for ch in range(2) for color in range(2)]
    came = {k: own_part(rows, 0, *k).astype(BF) for k in chains}
    rows, came = lax.optimization_barrier((rows, came))
    came = {k: ring(v, axes[k[1]][0]) for k, v in came.items()}
    for step in range(1, 3):
        for ch, color in chains:
            total = own_part(rows, step, ch, color) + came[ch, color].astype(F32)
            came[ch, color] = ring(total.astype(BF), axes[color][0])
    summed = []
    for color in range(2):
        parts = {}
        for r in turns:
            lo, hi = 32 * r, 32 * r + 32
            parts[r] = jnp.concatenate(
                [
                    own_part(rows, 3, ch, color, lo, hi) + came[ch, color][lo:hi].astype(F32)
                    for ch in range(2)
                ],
                axis=1,
            )
        total = parts[0]
        for r in (1, 2, 3):
            total += onward(parts[r].astype(BF), axes[color][1], -r).astype(F32)
        summed.append(total)
    summed = jnp.concatenate(summed)
    summed = (summed[:, :2048], summed[:, 2048:])
    tail = summed[1][:, 2048:]
    blocks = {
        1: summed[0][:, :1024],
        2: summed[0][:, 1024:],
        3: summed[1][:, :1024],
        0: summed[1][:, 1024:2048],
    }
    total = jnp.concatenate([blocks[0], tail], axis=1)
    for r in (1, 2, 3):
        total = total + send(
            jnp.concatenate([blocks[r], tail], axis=1).astype(BF), dx=r
        ).astype(F32)

    own_slot = jnp.sum(
        jnp.where(token_adapter[:, None] == names[None, :], adapter_slot_table[None, :], 0), axis=1
    )
    low_down = total[:, 1024:].astype(BF)
    ry = way * (y - own_slot // 8) % 4
    rz = way * (z - own_slot // 2 % 4) % 4
    at = jnp.arange(2048, dtype=jnp.int32) // 128
    spread = jnp.where((rz * 4 + ry)[:, None] == at[None, :], jnp.tile(low_down, (1, 16)), 0)
    delta = jnp.dot(spread, exits, preferred_element_type=F32)
    return (total[:, :1024] + delta).astype(BF)


def solution(mesh):
    return jax.shard_map(
        on_device,
        mesh=mesh,
        in_specs=(
            P("adapter", "tensor"),
            P("adapter"),
            P(),
            P(None, ("adapter", "tensor")),
            P(None, ("adapter", "tensor")),
            P(("adapter", "tensor"), None),
            P("adapter", None, None),
            P(None, None, ("adapter", "tensor")),
            P(None, None, ("adapter", "tensor")),
            P(None, ("adapter", "tensor"), None),
            P("adapter", None, "tensor"),
        ),
        out_specs=P("adapter", "tensor"),
        check_vma=False,
    )
```

```python
import functools

import jax
import jax.numpy as jnp
from jax import lax
from jax.experimental import pallas as pl
from jax.experimental.pallas import tpu as pltpu
from jax.sharding import PartitionSpec as P

SEGMENT = 80
BF = jnp.bfloat16
F32 = jnp.float32
AXES = ("adapter", "tensor")
VMEM_LIMIT = 60 * 1024 * 1024


def pairs(move):
    out = []
    for i in range(128):
        y, z, x, c = i // 32, (i // 8) % 4, (i // 2) % 4, i % 2
        ty, tz, tx, tc = move(y, z, x, c)
        out.append((i, (ty % 4) * 32 + (tz % 4) * 8 + (tx % 4) * 2 + tc % 2))
    return out


def send(value, dy=0, dz=0, dx=0, dc=0):
    return lax.ppermute(value, AXES, pairs(lambda y, z, x, c: (y + dy, z + dz, x + dx, c + dc)))


def onward(value, axis, step):
    def move(y, z, x, c):
        d = step * (1 - 2 * c)
        return (y + d, z, x, c) if axis == "y" else (y, z + d, x, c)

    return lax.ppermute(value, AXES, pairs(move))


def ring(value, axis):
    return onward(value, axis, 1)


def params(n=1):
    return pltpu.CompilerParams(
        dimension_semantics=("arbitrary",) * n, vmem_limit_bytes=VMEM_LIMIT
    )


def nt(a, b):
    return lax.dot_general(a, b, (((1,), (1,)), ((), ())), preferred_element_type=F32)


def low_kernel(x_ref, e_ref, s_ref, o_ref, acc):
    k = pl.program_id(0)

    @pl.when(k == 0)
    def _():
        acc[...] = jnp.zeros_like(acc)

    for j in range(2):
        x = x_ref[:, j].reshape(1024, 1024)
        at = pl.ds(1024 * j, 1024)
        e = jnp.concatenate([e_ref[0, at], e_ref[1, at]], axis=1)
        acc[...] += jnp.dot(x, e, preferred_element_type=F32)

    @pl.when(k == pl.num_programs(0) - 1)
    def _():
        for j in range(2):
            o_ref[j] = jnp.dot(
                s_ref[j], acc[:, 128 * j : 128 * (j + 1)].astype(BF), preferred_element_type=F32
            ).astype(BF)


def low_own_rows(every, entry, select):
    return pl.pallas_call(
        low_kernel,
        grid=(4,),
        in_specs=[
            pl.BlockSpec((16, 2, 64, 1024), lambda k: (0, k, 0, 0)),
            pl.BlockSpec((2, 2048, 128), lambda k: (0, k, 0)),
            pl.BlockSpec((2, SEGMENT, 1024), lambda k: (0, 0, 0)),
        ],
        out_specs=pl.BlockSpec((2, SEGMENT, 128), lambda k: (0, 0, 0)),
        out_shape=jax.ShapeDtypeStruct((2, SEGMENT, 128), BF),
        scratch_shapes=[pltpu.VMEM((1024, 256), F32)],
        compiler_params=params(),
        cost_estimate=pl.CostEstimate(
            flops=2 * 1024 * 8192 * 256, bytes_accessed=21 << 20, transcendentals=0
        ),
        name="low_own",
    )(every, entry, select)


def gate_up_kernel(x_ref, g_ref, u_ref, *refs):
    o_ref = refs[-1]
    n = g_ref.shape[0]

    @pl.when(pl.program_id(0) == 0)
    def _():
        o_ref[...] = jnp.zeros_like(o_ref)

    for j in range(2):
        x = x_ref[:, j].reshape(512, 1024)
        at = pl.ds(1024 * j, 1024)
        o_ref[0, :, :n] += nt(x, g_ref[:, at])
        o_ref[0, :, 256 : 256 + n] += nt(x, u_ref[:, at])


def gate_up(every, gate, up, half, sums):
    n = gate.shape[0]
    args = [every, gate, up]
    specs = [
        pl.BlockSpec((8, 2, 64, 1024), lambda k: (half, k, 0, 0)),
        pl.BlockSpec((n, 2048), lambda k: (0, k)),
        pl.BlockSpec((n, 2048), lambda k: (0, k)),
    ]
    if sums is not None:
        args.append(sums)
        specs.append(pl.BlockSpec(memory_space=pl.ANY))
    return pl.pallas_call(
        gate_up_kernel,
        grid=(4,),
        in_specs=specs,
        out_specs=pl.BlockSpec((1, 512, 512), lambda k: (half, 0, 0)),
        out_shape=jax.ShapeDtypeStruct((2, 512, 512), F32),
        input_output_aliases={} if sums is None else {3: 0},
        compiler_params=params(),
        cost_estimate=pl.CostEstimate(
            flops=1024 * 8192 * 512, bytes_accessed=16 << 20, transcendentals=0
        ),
        name="gate_up",
    )(*args)


def hidden_kernel(
    place, a_ref, slot_ref, row_ref, low_ref, ge_ref, ue_ref, de_ref, h_ref, t_ref
):
    lane = lax.broadcasted_iota(jnp.int32, (256, 256), 1)
    row = row_ref[...]
    slot = slot_ref[...]

    def equal(value, index):
        return jnp.where(value == index, 1.0, 0.0)

    low = jnp.zeros((256, 128), F32)
    for j in range(10):
        pick = equal(row, lane + 256 * j).astype(BF)
        low += jnp.dot(pick, low_ref[pl.ds(256 * j, 256)], preferred_element_type=F32)
    lg = low[:, :64].astype(BF)
    lu = low[:, 64:].astype(BF)
    lg = jnp.concatenate([lg] * 4, axis=1)
    lu = jnp.concatenate([lu] * 4, axis=1)
    n = ge_ref.shape[1]
    gate = a_ref[0, :, :n]
    up = a_ref[0, :, 256 : 256 + n]
    for j in range(8):
        mask = equal(slot, lane // 64 + 4 * j).astype(BF)
        gate += jnp.dot(lg * mask, ge_ref[pl.ds(256 * j, 256)], preferred_element_type=F32)
        up += jnp.dot(lu * mask, ue_ref[pl.ds(256 * j, 256)], preferred_element_type=F32)
    hidden = (gate / (1.0 + jnp.exp(-gate)) * up).astype(BF)
    down = jnp.zeros((256, 256), F32)
    for j in range(8):
        mask = equal(slot, lane // 64 + 4 * j)
        down += nt(hidden, de_ref[pl.ds(256 * j, 256)]) * mask
    down = (down[:, :128] + down[:, 128:]).astype(BF)
    wide = jnp.concatenate([hidden, jnp.zeros((256, 256 - hidden.shape[1]), BF), down], axis=1)
    ry = place[pl.program_id(0)]
    for z in range(4):
        rz = place[4 + z]
        upper = wide[64 * z : 64 * z + 32]
        lower = wide[64 * z + 32 : 64 * z + 64]
        h_ref[(rz + 3) % 4, 0, ry] = upper
        h_ref[(ry + 3) % 4, 1, rz] = lower
        t_ref[(7 - rz) % 4, 0, (4 - ry) % 4] = upper
        t_ref[(7 - ry) % 4, 1, (4 - rz) % 4] = lower


def hidden_rows(place, sums, slot, row, low, gate_exit, up_exit, down_entry):
    n = gate_exit.shape[1]
    return pl.pallas_call(
        hidden_kernel,
        grid_spec=pltpu.PrefetchScalarGridSpec(
            num_scalar_prefetch=1,
            grid=(4,),
            in_specs=[
                pl.BlockSpec((1, 256, 512), lambda i, p: (i, 0, 0)),
                pl.BlockSpec((256, 1), lambda i, p: (i, 0)),
                pl.BlockSpec((256, 1), lambda i, p: (i, 0)),
                pl.BlockSpec((2560, 128), lambda i, p: (0, 0)),
                pl.BlockSpec((2048, n), lambda i, p: (0, 0)),
                pl.BlockSpec((2048, n), lambda i, p: (0, 0)),
                pl.BlockSpec((2048, n), lambda i, p: (0, 0)),
            ],
            out_specs=[pl.BlockSpec((4, 2, 4, 32, 384), lambda i, p: (0, 0, 0, 0, 0))] * 2,
        ),
        out_shape=[jax.ShapeDtypeStruct((4, 2, 4, 32, 384), BF)] * 2,
        compiler_params=params(),
        cost_estimate=pl.CostEstimate(
            flops=2 * 1024 * 2560 * 512, bytes_accessed=16 << 20, transcendentals=1024 * n
        ),
        name="hidden_rows",
    )(place, sums, slot, row, low, gate_exit, up_exit, down_entry)


def on_device(
    tokens,
    token_adapter,
    adapter_slot_table,
    gate_matrix,
    up_matrix,
    down_matrix,
    adapter_entry_maps,
    adapter_gate_exit,
    adapter_up_exit,
    adapter_down_entry,
    adapter_down_exit,
):
    units = gate_matrix.shape[1]
    a = lax.axis_index("adapter")
    t = lax.axis_index("tensor")
    y, z, x, c = a // 4, a % 4, t // 2, t % 2
    way = 1 - 2 * c

    every = lax.all_gather(tokens, AXES, axis=0, tiled=False).reshape(16, 8, 64, 1024)
    ids = lax.all_gather(token_adapter, "adapter", axis=0, tiled=True)

    exits = adapter_down_exit
    for axis in "yz":
        exits = [exits]
        for _ in range(3):
            exits.append(ring(exits[-1], axis))
        if axis == "y":
            exits = jnp.stack(exits)

    names = jnp.arange(32, dtype=jnp.int32)
    member = ids[:, None] == names[None, :]
    order = jnp.arange(1024, dtype=jnp.int32)
    before = (order[:, None] > order[None, :]).astype(BF)
    earlier = jnp.dot(before, member.astype(BF), preferred_element_type=F32).astype(jnp.int32)
    rank_in = jnp.sum(jnp.where(member, earlier, 0), axis=1)
    slot = jnp.sum(jnp.where(member, adapter_slot_table[None, :], 0), axis=1)
    owner = slot // 2
    row = (slot % 2) * SEGMENT + rank_in
    select = (
        (jnp.where(owner == a, row, -1))[None, :] == jnp.arange(160, dtype=jnp.int32)[:, None]
    ).astype(BF).reshape(2, SEGMENT, 1024)
    relative = ((owner % 4 - z) % 4) * 4 + (owner // 4 - y) % 4

    def column(r, core):
        at = ((x + r) % 4 * 2 + core) * 1024
        return lax.dynamic_slice(down_matrix, (0, at), (units, 1024))

    turns = (1, 2, 3, 0)
    def columns(turns, core, rows, extra):
        width = 1024 * len(turns)
        if extra:
            out = jnp.pad(jnp.eye(128, dtype=BF), ((rows - 128, 0), (width, 0)))
        else:
            out = jnp.zeros((rows, width), BF)
        for i, r in enumerate(turns):
            out = lax.dynamic_update_slice(out, column(r, core), (0, 1024 * i))
        return out

    theirs = columns(turns, 1 - c, 384, True)
    mine = (columns((1, 2), c, 256, False), columns((3, 0), c, 384, True))

    every, select, slot, row, theirs, mine = lax.optimization_barrier(
        (every, select, slot, (relative * 160 + row)[:, None], theirs, mine)
    )
    low_own = low_own_rows(every, adapter_entry_maps, select).reshape(160, 128)
    low_own, exits = lax.optimization_barrier((low_own, exits))
    exits = jnp.stack(exits).reshape(2048, 1024)
    low = jnp.stack([low_own] + [send(low_own, dy=-d) for d in (1, 2, 3)])
    low = jnp.stack([low] + [send(low, dz=-d) for d in (1, 2, 3)]).reshape(2560, 128)
    sums = None
    for half in range(2):
        sums = gate_up(every, gate_matrix.T, up_matrix.T, half, sums)
    sums = sums.reshape(4, 256, 512)

    quarter = jnp.arange(4, dtype=jnp.int32)
    place = jnp.concatenate([way * (y - quarter) % 4, way * (z - quarter) % 4])
    rows, back = hidden_rows(
        place,
        sums,
        slot[:, None],
        row,
        low,
        adapter_gate_exit.reshape(2048, units),
        adapter_up_exit.reshape(2048, units),
        adapter_down_entry.transpose(0, 2, 1).reshape(2048, units),
    )
    rows = rows.reshape(4, 2, 128, 384)
    back = back.reshape(4, 256, 384)
    first = jnp.dot(back[0], theirs, preferred_element_type=F32).astype(BF)
    back, first = lax.optimization_barrier((back, first))
    rest = jnp.dot(back[1:].reshape(768, 384), theirs, preferred_element_type=F32).astype(BF)
    rest, first_other = lax.optimization_barrier((rest, send(first, dc=1)))
    others = jnp.split(send(rest, dc=1).reshape(3, 2, 128, 4224), 3)
    others = [first_other.reshape(1, 2, 128, 4224)] + others

    axes = (("z", "y"), ("y", "z"))
    spans = ((0, 2048), (2048, 4224))

    def own_part(rows, step, ch, color, lo=0, hi=128):
        h = rows[step, color, lo:hi, : mine[ch].shape[0]]
        part = jnp.dot(h, mine[ch], preferred_element_type=F32)
        return part + others[step][0, color, lo:hi, slice(*spans[ch])].astype(F32)

    chains = [(ch, color) for ch in range(2) for color in range(2)]
    came = {k: own_part(rows, 0, *k).astype(BF) for k in chains}
    rows, came = lax.optimization_barrier((rows, came))
    came = {k: ring(v, axes[k[1]][0]) for k, v in came.items()}
    for step in range(1, 3):
        for ch, color in chains:
            total = own_part(rows, step, ch, color) + came[ch, color].astype(F32)
            came[ch, color] = ring(total.astype(BF), axes[color][0])
    summed = []
    for color in range(2):
        parts = {}
        for r in turns:
            lo, hi = 32 * r, 32 * r + 32
            parts[r] = jnp.concatenate(
                [
                    own_part(rows, 3, ch, color, lo, hi) + came[ch, color][lo:hi].astype(F32)
                    for ch in range(2)
                ],
                axis=1,
            )
        total = parts[0]
        for r in (1, 2, 3):
            total += onward(parts[r].astype(BF), axes[color][1], -r).astype(F32)
        summed.append(total)
    summed = jnp.concatenate(summed)
    summed = (summed[:, :2048], summed[:, 2048:])
    tail = summed[1][:, 2048:]
    blocks = {
        1: summed[0][:, :1024],
        2: summed[0][:, 1024:],
        3: summed[1][:, :1024],
        0: summed[1][:, 1024:2048],
    }
    total = jnp.concatenate([blocks[0], tail], axis=1)
    for r in (1, 2, 3):
        total = total + send(
            jnp.concatenate([blocks[r], tail], axis=1).astype(BF), dx=r
        ).astype(F32)

    own_slot = jnp.sum(
        jnp.where(token_adapter[:, None] == names[None, :], adapter_slot_table[None, :], 0), axis=1
    )
    low_down = total[:, 1024:].astype(BF)
    ry = way * (y - own_slot // 8) % 4
    rz = way * (z - own_slot // 2 % 4) % 4
    at = jnp.arange(2048, dtype=jnp.int32) // 128
    spread = jnp.where((rz * 4 + ry)[:, None] == at[None, :], jnp.tile(low_down, (1, 16)), 0)
    delta = jnp.dot(spread, exits, preferred_element_type=F32)
    return (total[:, :1024] + delta).astype(BF)


def solution(mesh):
    return jax.shard_map(
        on_device,
        mesh=mesh,
        in_specs=(
            P("adapter", "tensor"),
            P("adapter"),
            P(),
            P(None, ("adapter", "tensor")),
            P(None, ("adapter", "tensor")),
            P(("adapter", "tensor"), None),
            P("adapter", None, None),
            P(None, None, ("adapter", "tensor")),
            P(None, None, ("adapter", "tensor")),
            P(None, ("adapter", "tensor"), None),
            P("adapter", None, "tensor"),
        ),
        out_specs=P("adapter", "tensor"),
        check_vma=False,
    )
```

```python
import functools

import jax
import jax.numpy as jnp
from jax import lax
from jax.experimental import pallas as pl
from jax.experimental.pallas import tpu as pltpu
from jax.sharding import PartitionSpec as P

SEGMENT = 80
BF = jnp.bfloat16
F32 = jnp.float32
AXES = ("adapter", "tensor")
VMEM_LIMIT = 60 * 1024 * 1024


def pairs(move):
    out = []
    for i in range(128):
        y, z, x, c = i // 32, (i // 8) % 4, (i // 2) % 4, i % 2
        ty, tz, tx, tc = move(y, z, x, c)
        out.append((i, (ty % 4) * 32 + (tz % 4) * 8 + (tx % 4) * 2 + tc % 2))
    return out


def send(value, dy=0, dz=0, dx=0, dc=0):
    return lax.ppermute(value, AXES, pairs(lambda y, z, x, c: (y + dy, z + dz, x + dx, c + dc)))


def onward(value, axis, step):
    def move(y, z, x, c):
        d = step * (1 - 2 * c)
        return (y + d, z, x, c) if axis == "y" else (y, z + d, x, c)

    return lax.ppermute(value, AXES, pairs(move))


def ring(value, axis):
    return onward(value, axis, 1)


def params(n=1):
    return pltpu.CompilerParams(
        dimension_semantics=("arbitrary",) * n, vmem_limit_bytes=VMEM_LIMIT
    )


def nt(a, b):
    return lax.dot_general(a, b, (((1,), (1,)), ((), ())), preferred_element_type=F32)


def low_kernel(x_ref, e_ref, s_ref, o_ref, acc):
    k = pl.program_id(0)

    @pl.when(k == 0)
    def _():
        acc[...] = jnp.zeros_like(acc)

    for j in range(2):
        x = x_ref[:, j].reshape(1024, 1024)
        at = pl.ds(1024 * j, 1024)
        e = jnp.concatenate([e_ref[0, at], e_ref[1, at]], axis=1)
        acc[...] += jnp.dot(x, e, preferred_element_type=F32)

    @pl.when(k == pl.num_programs(0) - 1)
    def _():
        for j in range(2):
            o_ref[j] = jnp.dot(
                s_ref[j], acc[:, 128 * j : 128 * (j + 1)].astype(BF), preferred_element_type=F32
            ).astype(BF)


def low_own_rows(every, entry, select):
    return pl.pallas_call(
        low_kernel,
        grid=(4,),
        in_specs=[
            pl.BlockSpec((16, 2, 64, 1024), lambda k: (0, k, 0, 0)),
            pl.BlockSpec((2, 2048, 128), lambda k: (0, k, 0)),
            pl.BlockSpec((2, SEGMENT, 1024), lambda k: (0, 0, 0)),
        ],
        out_specs=pl.BlockSpec((2, SEGMENT, 128), lambda k: (0, 0, 0)),
        out_shape=jax.ShapeDtypeStruct((2, SEGMENT, 128), BF),
        scratch_shapes=[pltpu.VMEM((1024, 256), F32)],
        compiler_params=params(),
        cost_estimate=pl.CostEstimate(
            flops=2 * 1024 * 8192 * 256, bytes_accessed=21 << 20, transcendentals=0
        ),
        name="low_own",
    )(every, entry, select)


def gate_up_kernel(x_ref, g_ref, u_ref, *refs):
    o_ref = refs[-1]
    n = g_ref.shape[0]

    @pl.when(pl.program_id(0) == 0)
    def _():
        o_ref[...] = jnp.zeros_like(o_ref)

    for j in range(2):
        x = x_ref[:, j].reshape(512, 1024)
        at = pl.ds(1024 * j, 1024)
        o_ref[0, :, :n] += nt(x, g_ref[:, at])
        o_ref[0, :, 256 : 256 + n] += nt(x, u_ref[:, at])


def gate_up(every, gate, up, half, sums):
    n = gate.shape[0]
    args = [every, gate, up]
    specs = [
        pl.BlockSpec((8, 2, 64, 1024), lambda k: (half, k, 0, 0)),
        pl.BlockSpec((n, 2048), lambda k: (0, k)),
        pl.BlockSpec((n, 2048), lambda k: (0, k)),
    ]
    if sums is not None:
        args.append(sums)
        specs.append(pl.BlockSpec(memory_space=pl.ANY))
    return pl.pallas_call(
        gate_up_kernel,
        grid=(4,),
        in_specs=specs,
        out_specs=pl.BlockSpec((1, 512, 512), lambda k: (half, 0, 0)),
        out_shape=jax.ShapeDtypeStruct((2, 512, 512), F32),
        input_output_aliases={} if sums is None else {3: 0},
        compiler_params=params(),
        cost_estimate=pl.CostEstimate(
            flops=1024 * 8192 * 512, bytes_accessed=16 << 20, transcendentals=0
        ),
        name="gate_up",
    )(*args)


def hidden_kernel(
    place, a_ref, slot_ref, row_ref, low_ref, ge_ref, ue_ref, de_ref, h_ref, t_ref
):
    lane = lax.broadcasted_iota(jnp.int32, (256, 256), 1)
    row = row_ref[...]
    slot = slot_ref[...]

    def equal(value, index):
        return jnp.where(value == index, 1.0, 0.0)

    low = jnp.zeros((256, 128), F32)
    for j in range(10):
        pick = equal(row, lane + 256 * j).astype(BF)
        low += jnp.dot(pick, low_ref[pl.ds(256 * j, 256)], preferred_element_type=F32)
    lg = low[:, :64].astype(BF)
    lu = low[:, 64:].astype(BF)
    lg = jnp.concatenate([lg] * 4, axis=1)
    lu = jnp.concatenate([lu] * 4, axis=1)
    n = ge_ref.shape[1]
    gate = a_ref[0, :, :n]
    up = a_ref[0, :, 256 : 256 + n]
    for j in range(8):
        mask = equal(slot, lane // 64 + 4 * j).astype(BF)
        gate += jnp.dot(lg * mask, ge_ref[pl.ds(256 * j, 256)], preferred_element_type=F32)
        up += jnp.dot(lu * mask, ue_ref[pl.ds(256 * j, 256)], preferred_element_type=F32)
    hidden = (gate / (1.0 + jnp.exp(-gate)) * up).astype(BF)
    down = jnp.zeros((256, 256), F32)
    for j in range(8):
        mask = equal(slot, lane // 64 + 4 * j)
        down += nt(hidden, de_ref[pl.ds(256 * j, 256)]) * mask
    down = (down[:, :128] + down[:, 128:]).astype(BF)
    wide = jnp.concatenate([hidden, jnp.zeros((256, 256 - hidden.shape[1]), BF), down], axis=1)
    ry = place[pl.program_id(0)]
    for z in range(4):
        rz = place[4 + z]
        upper = wide[64 * z : 64 * z + 32]
        lower = wide[64 * z + 32 : 64 * z + 64]
        h_ref[(rz + 3) % 4, 0, ry] = upper
        h_ref[(ry + 3) % 4, 1, rz] = lower
        t_ref[(7 - rz) % 4, 0, (4 - ry) % 4] = upper
        t_ref[(7 - ry) % 4, 1, (4 - rz) % 4] = lower


def hidden_rows(place, sums, slot, row, low, gate_exit, up_exit, down_entry):
    n = gate_exit.shape[1]
    return pl.pallas_call(
        hidden_kernel,
        grid_spec=pltpu.PrefetchScalarGridSpec(
            num_scalar_prefetch=1,
            grid=(4,),
            in_specs=[
                pl.BlockSpec((1, 256, 512), lambda i, p: (i, 0, 0)),
                pl.BlockSpec((256, 1), lambda i, p: (i, 0)),
                pl.BlockSpec((256, 1), lambda i, p: (i, 0)),
                pl.BlockSpec((2560, 128), lambda i, p: (0, 0)),
                pl.BlockSpec((2048, n), lambda i, p: (0, 0)),
                pl.BlockSpec((2048, n), lambda i, p: (0, 0)),
                pl.BlockSpec((2048, n), lambda i, p: (0, 0)),
            ],
            out_specs=[pl.BlockSpec((4, 2, 4, 32, 384), lambda i, p: (0, 0, 0, 0, 0))] * 2,
        ),
        out_shape=[jax.ShapeDtypeStruct((4, 2, 4, 32, 384), BF)] * 2,
        compiler_params=params(),
        cost_estimate=pl.CostEstimate(
            flops=2 * 1024 * 2560 * 512, bytes_accessed=16 << 20, transcendentals=1024 * n
        ),
        name="hidden_rows",
    )(place, sums, slot, row, low, gate_exit, up_exit, down_entry)


def on_device(
    tokens,
    token_adapter,
    adapter_slot_table,
    gate_matrix,
    up_matrix,
    down_matrix,
    adapter_entry_maps,
    adapter_gate_exit,
    adapter_up_exit,
    adapter_down_entry,
    adapter_down_exit,
):
    units = gate_matrix.shape[1]
    a = lax.axis_index("adapter")
    t = lax.axis_index("tensor")
    y, z, x, c = a // 4, a % 4, t // 2, t % 2
    way = 1 - 2 * c

    every = lax.all_gather(tokens, AXES, axis=0, tiled=False).reshape(16, 8, 64, 1024)
    ids = lax.all_gather(token_adapter, "adapter", axis=0, tiled=True)

    exits = adapter_down_exit
    for axis in "yz":
        exits = [exits]
        for _ in range(3):
            exits.append(ring(exits[-1], axis))
        if axis == "y":
            exits = jnp.stack(exits)

    names = jnp.arange(32, dtype=jnp.int32)
    member = ids[:, None] == names[None, :]
    order = jnp.arange(1024, dtype=jnp.int32)
    before = (order[:, None] > order[None, :]).astype(BF)
    earlier = jnp.dot(before, member.astype(BF), preferred_element_type=F32).astype(jnp.int32)
    rank_in = jnp.sum(jnp.where(member, earlier, 0), axis=1)
    slot = jnp.sum(jnp.where(member, adapter_slot_table[None, :], 0), axis=1)
    owner = slot // 2
    row = (slot % 2) * SEGMENT + rank_in
    select = (
        (jnp.where(owner == a, row, -1))[None, :] == jnp.arange(160, dtype=jnp.int32)[:, None]
    ).astype(BF).reshape(2, SEGMENT, 1024)
    relative = ((owner % 4 - z) % 4) * 4 + (owner // 4 - y) % 4

    def column(r, core):
        at = ((x + r) % 4 * 2 + core) * 1024
        return lax.dynamic_slice(down_matrix, (0, at), (units, 1024))

    turns = (1, 2, 3, 0)
    def columns(turns, core, rows, extra):
        width = 1024 * len(turns)
        if extra:
            out = jnp.pad(jnp.eye(128, dtype=BF), ((rows - 128, 0), (width, 0)))
        else:
            out = jnp.zeros((rows, width), BF)
        for i, r in enumerate(turns):
            out = lax.dynamic_update_slice(out, column(r, core), (0, 1024 * i))
        return out

    theirs = columns(turns, 1 - c, 384, True)
    mine = (columns((1, 2), c, 256, False), columns((3, 0), c, 384, True))

    every, exits, select, slot, row, theirs, mine = lax.optimization_barrier(
        (every, exits, select, slot, (relative * 160 + row)[:, None], theirs, mine)
    )
    low_own = low_own_rows(every, adapter_entry_maps, select).reshape(160, 128)
    exits = jnp.stack(exits).reshape(2048, 1024)
    low = jnp.stack([low_own] + [send(low_own, dy=-d) for d in (1, 2, 3)])
    low = jnp.stack([low] + [send(low, dz=-d) for d in (1, 2, 3)]).reshape(2560, 128)
    sums = None
    for half in range(2):
        sums = gate_up(every, gate_matrix.T, up_matrix.T, half, sums)
    sums = sums.reshape(4, 256, 512)

    quarter = jnp.arange(4, dtype=jnp.int32)
    place = jnp.concatenate([way * (y - quarter) % 4, way * (z - quarter) % 4])
    rows, back = hidden_rows(
        place,
        sums,
        slot[:, None],
        row,
        low,
        adapter_gate_exit.reshape(2048, units),
        adapter_up_exit.reshape(2048, units),
        adapter_down_entry.transpose(0, 2, 1).reshape(2048, units),
    )
    rows = rows.reshape(4, 2, 128, 384)
    back = back.reshape(4, 256, 384)
    first = jnp.dot(back[0], theirs, preferred_element_type=F32).astype(BF)
    back, first = lax.optimization_barrier((back, first))
    rest = jnp.dot(back[1:].reshape(768, 384), theirs, preferred_element_type=F32).astype(BF)
    rest, first_other = lax.optimization_barrier((rest, send(first, dc=1)))
    others = jnp.split(send(rest, dc=1).reshape(3, 2, 128, 4224), 3)
    others = [first_other.reshape(1, 2, 128, 4224)] + others

    axes = (("z", "y"), ("y", "z"))
    spans = ((0, 2048), (2048, 4224))

    def own_part(rows, step, ch, color, lo=0, hi=128):
        h = rows[step, color, lo:hi, : mine[ch].shape[0]]
        part = jnp.dot(h, mine[ch], preferred_element_type=F32)
        return part + others[step][0, color, lo:hi, slice(*spans[ch])].astype(F32)

    chains = [(ch, color) for ch in range(2) for color in range(2)]
    came = {k: own_part(rows, 0, *k).astype(BF) for k in chains}
    rows, came = lax.optimization_barrier((rows, came))
    came = {k: ring(v, axes[k[1]][0]) for k, v in came.items()}
    for step in range(1, 3):
        for ch, color in chains:
            total = own_part(rows, step, ch, color) + came[ch, color].astype(F32)
            came[ch, color] = ring(total.astype(BF), axes[color][0])
    summed = []
    for color in range(2):
        parts = {}
        for r in turns:
            lo, hi = 32 * r, 32 * r + 32
            parts[r] = jnp.concatenate(
                [
                    own_part(rows, 3, ch, color, lo, hi) + came[ch, color][lo:hi].astype(F32)
                    for ch in range(2)
                ],
                axis=1,
            )
        total = parts[0]
        for r in (1, 2, 3):
            total += onward(parts[r].astype(BF), axes[color][1], -r).astype(F32)
        summed.append(total)
    summed = jnp.concatenate(summed)
    summed = (summed[:, :2048], summed[:, 2048:])
    tail = summed[1][:, 2048:]
    blocks = {
        1: summed[0][:, :1024],
        2: summed[0][:, 1024:],
        3: summed[1][:, :1024],
        0: summed[1][:, 1024:2048],
    }
    total = jnp.concatenate([blocks[0], tail], axis=1)
    for r in (1, 2, 3):
        total = total + send(
            jnp.concatenate([blocks[r], tail], axis=1).astype(BF), dx=r
        ).astype(F32)

    own_slot = jnp.sum(
        jnp.where(token_adapter[:, None] == names[None, :], adapter_slot_table[None, :], 0), axis=1
    )
    low_down = total[:, 1024:].astype(BF)
    ry = way * (y - own_slot // 8) % 4
    rz = way * (z - own_slot // 2 % 4) % 4
    at = jnp.arange(2048, dtype=jnp.int32) // 128
    spread = jnp.where((rz * 4 + ry)[:, None] == at[None, :], jnp.tile(low_down, (1, 16)), 0)
    delta = jnp.dot(spread, exits, preferred_element_type=F32)
    return (total[:, :1024] + delta).astype(BF)


def solution(mesh):
    return jax.shard_map(
        on_device,
        mesh=mesh,
        in_specs=(
            P("adapter", "tensor"),
            P("adapter"),
            P(),
            P(None, ("adapter", "tensor")),
            P(None, ("adapter", "tensor")),
            P(("adapter", "tensor"), None),
            P("adapter", None, None),
            P(None, None, ("adapter", "tensor")),
            P(None, None, ("adapter", "tensor")),
            P(None, ("adapter", "tensor"), None),
            P("adapter", None, "tensor"),
        ),
        out_specs=P("adapter", "tensor"),
        check_vma=False,
    )
```
